32 devices in a mesh: grp: 2 (over y), stn: 16 (over z, x, core).
Axes of the slice: x: 2, y: 2, z: 4, core: 2. Of those that a mesh axis runs over, the one named last changes fastest.
Arguments:
- pair_uvw_coordinates: float32 [3, 4096], P(None, ('grp', 'stn')), parts along dimension 1, may hold values from -120 to 120
- directions: float32 [2, 128], replicated, may hold values from -0.4 to 0.4
- brightness: float32 [8, 32, 128], replicated, may hold values from -0.4 to 0.4
- observed: float32 [32, 8, 4096], P(None, None, ('grp', 'stn')), parts along dimension 2, may hold values from -6 to 6
- coefficients: float32 [64, 24, 128], P(('grp', 'stn')), parts along dimension 0, may hold values from -1.5 to 2.5
- station_pair: int32 [2, 4096], P(None, ('grp', 'stn')), parts along dimension 1, may hold values from 0 to 31, as said below
Outputs:
- gradient: float32 [64, 24, 128], P(('grp', 'stn')), parts along dimension 0
- residual: float32 [32, 8, 4096], P(None, None, ('grp', 'stn')), parts along dimension 2
The draws below stay inside these ranges and needn't reach their ends.
There are 2 independent parts, one for each index of `grp`. The reference program is written for one: setup_inputs(seed, part) draws one part's arguments, and reference() takes and returns one part's arrays. A program takes and returns all parts, laid end to end along the dimension named above; an argument that names none is the same for every part. Nothing has to cross between parts.
Inputs may be any that keep to these rules, and one draw needn't show every extreme that they name: `station_pair`: the two stations of a baseline differ.
All inputs are finite; a program needn't handle non-finite values.
Results may differ from the reference program's by a relative error of at most 0.0003.
Values sent between devices are 32-bit elements; how exact they have to be, the bound alone decides.
A program may use at most 128 MiB of HBM per device.

```python
import math
import jax
import jax.numpy as jnp
from jax import lax

ANTENNAS_HELD = 2
K = 128
CHANNEL_TOTAL = 32
NP = 3
PAIRS_IN_TILE = 1
NS = 32
ANTENNA_PAIRS = 2048
N_STN = 16


def draw_coefficients(key, part):
    key = jax.random.fold_in(key, 11)
    noise_part = 0.25 * jnp.clip(jax.random.normal(key, (NS, NP, 8, K), jnp.float32), -6.0, 6.0)
    degree_pos = jnp.arange(NP)[None, :, None, None]
    comp_pos = jnp.arange(8)[None, None, :, None]
    identity_part = jnp.where((degree_pos == 0) & ((comp_pos == 0) | (comp_pos == 6)), 1.0, 0.0)
    return (noise_part + identity_part).astype(jnp.float32).reshape(NS, NP * 8, K)


def draw_station_pair(key, part):
    key = jax.random.fold_in(key, 23)
    seed_divisions = jax.random.split(key, 4)
    tile_number = ANTENNA_PAIRS // PAIRS_IN_TILE
    front_partition = jax.random.randint(seed_divisions[0], (tile_number,), 0, N_STN)
    group_offset = jax.random.randint(seed_divisions[1], (tile_number,), 1, N_STN)
    back_partition = (front_partition + group_offset) % N_STN
    first_antenna = jnp.repeat(front_partition, PAIRS_IN_TILE) * ANTENNAS_HELD + jax.random.randint(seed_divisions[2], (ANTENNA_PAIRS,), 0, ANTENNAS_HELD)
    second_antenna = jnp.repeat(back_partition, PAIRS_IN_TILE) * ANTENNAS_HELD + jax.random.randint(seed_divisions[3], (ANTENNA_PAIRS,), 0, ANTENNAS_HELD)
    first_antenna = first_antenna.at[0].set(0)
    second_antenna = second_antenna.at[0].set(NS - 1)
    return jnp.stack((first_antenna, second_antenna)).astype(jnp.int32)


def block_scale(stream_key, extent, shards, low, top_value):
    level = 1.0
    for dim, parts in shards:
        heights = jax.random.uniform(jax.random.fold_in(jax.random.fold_in(stream_key, 6), dim), (parts,), jnp.float32, low / len(shards), top_value / len(shards))
        level = level * jnp.repeat(jnp.exp(heights), extent[dim] // parts).reshape((-1,) + (1,) * (len(extent) - 1 - dim))
    return level


def scatter_about(rng, extent, spread, reach, cuts=(), kind=jnp.bfloat16):
    gain = block_scale(rng, extent, cuts, -0.22, 0.18) if cuts else 1.0
    values = jax.random.normal(rng, extent, jnp.float32) * spread * gain
    return jnp.minimum(jnp.maximum(values, -reach), reach).astype(kind)


def setup_inputs(seed: int = 0, part: int = 0) -> dict:
    key_of = jax.random.split(jax.random.key(seed), 7)
    own_keys = jax.random.split(jax.random.fold_in(key_of[6], part), 7)
    pair_uvw_coordinates = scatter_about(own_keys[0], (3, ANTENNA_PAIRS), 20.0, 120.0, ((1, 16),), jnp.float32)
    directions = jnp.clip(jax.random.uniform(key_of[1], (2, K), jnp.float32, -0.4, 0.4), -0.4, 0.4)
    brightness = scatter_about(key_of[2], (8, CHANNEL_TOTAL, K), 0.0625, 0.4, (), jnp.float32)
    observed = scatter_about(own_keys[3], (CHANNEL_TOTAL, 8, ANTENNA_PAIRS), 1.0, 6.0, ((2, 16),), jnp.float32)
    coefficients = draw_coefficients(jax.random.fold_in(jax.random.fold_in(key_of[6], part), 71), part)
    station_pair = draw_station_pair(jax.random.fold_in(jax.random.fold_in(key_of[6], part), 71), part)
    return {"pair_uvw_coordinates": pair_uvw_coordinates, "directions": directions, "brightness": brightness, "observed": observed, "coefficients": coefficients, "station_pair": station_pair}


def powers_of(frequency_number, degree_count):
    channel_pos = jnp.arange(frequency_number, dtype=jnp.float32)
    centre = (2.0 * channel_pos - (frequency_number - 1)) / max(frequency_number - 1, 1)
    levels = [jnp.ones_like(centre)]
    for degree in range(1, degree_count):
        levels.append(levels[-1] * centre)
    return (jnp.stack(levels), 1.0 + 0.25 * centre)

def evaluate(coeff_table, powers):
    degree_count = powers.shape[0]
    shaped = coeff_table.reshape(coeff_table.shape[0], degree_count, 8, coeff_table.shape[2])
    result = shaped[:, 0][:, None] * powers[0][None, :, None, None]
    for degree in range(1, degree_count):
        result = result + shaped[:, degree][:, None] * powers[degree][None, :, None, None]
    return result

def contract(grads, powers):
    pieces = [lax.optimization_barrier(jnp.sum(grads * powers[degree][None, :, None, None], axis=1)) for degree in range(powers.shape[0])]
    stacked = jnp.stack(pieces, axis=1)
    return stacked.reshape(stacked.shape[0], stacked.shape[1] * 8, stacked.shape[3])

def mat_product(left_re, left_im, right_re, right_im):
    first_re = left_re[:, 0:1] * right_re[0:1] - left_im[:, 0:1] * right_im[0:1]
    second_re = left_re[:, 1:2] * right_re[1:2] - left_im[:, 1:2] * right_im[1:2]
    first_im = left_re[:, 0:1] * right_im[0:1] + left_im[:, 0:1] * right_re[0:1]
    second_im = left_re[:, 1:2] * right_im[1:2] + left_im[:, 1:2] * right_re[1:2]
    return (first_re + second_re, first_im + second_im)

def adjoint(matrix_re, matrix_im):
    return (jnp.swapaxes(matrix_re, 0, 1), -jnp.swapaxes(matrix_im, 0, 1))

def to_matrix(jones_rows):
    shaped = jones_rows.reshape(jones_rows.shape[0], jones_rows.shape[1], 2, 2, 2, jones_rows.shape[3])
    real_part = jnp.transpose(shaped[:, :, :, :, 0], (2, 3, 0, 1, 4))
    imag_part = jnp.transpose(shaped[:, :, :, :, 1], (2, 3, 0, 1, 4))
    return (real_part, imag_part)

def from_matrix(real_part, imag_part):
    stacked = jnp.stack((real_part, imag_part), axis=2)
    reordered = jnp.transpose(stacked, (3, 4, 0, 1, 2, 5))
    return reordered.reshape(reordered.shape[0], reordered.shape[1], 8, reordered.shape[5])

def baseline_terms(jones_near, jones_far, coords, directions, brightness, observed, freq_ratio):
    frequency_number = brightness.shape[1]
    dir_count = brightness.shape[2]
    entries_in_tile = coords.shape[1]
    depth_term = jnp.sqrt(1.0 - directions[0] * directions[0] - directions[1] * directions[1]) - 1.0
    inner_sum = coords[0][:, None] * directions[0][None, :] + coords[1][:, None] * directions[1][None, :] + coords[2][:, None] * depth_term[None, :]
    phase_angle = 2.0 * math.pi * freq_ratio[None, :, None] * inner_sum[:, None, :]
    cosine = jnp.cos(phase_angle)
    sine_part = jnp.sin(phase_angle)
    bright = brightness.reshape(2, 2, 2, frequency_number, dir_count)
    bright_re = bright[:, :, 0][:, :, None]
    bright_im = bright[:, :, 1][:, :, None]
    coh_re = bright_re * cosine + bright_im * sine_part
    coh_im = bright_im * cosine - bright_re * sine_part
    near_re, near_im = to_matrix(jones_near)
    far_re, far_im = to_matrix(jones_far)
    left_re, left_im = mat_product(near_re, near_im, coh_re, coh_im)
    fadj_re, fadj_im = adjoint(far_re, far_im)
    model_re, model_im = mat_product(left_re, left_im, fadj_re, fadj_im)
    cadj_re, cadj_im = adjoint(coh_re, coh_im)
    right_re, right_im = mat_product(far_re, far_im, cadj_re, cadj_im)
    seen_block = observed.reshape(frequency_number, 2, 2, 2, entries_in_tile)
    diff_re = jnp.transpose(seen_block[:, :, :, 0], (1, 2, 3, 0)) - lax.optimization_barrier(jnp.sum(model_re, axis=-1))
    diff_im = jnp.transpose(seen_block[:, :, :, 1], (1, 2, 3, 0)) - lax.optimization_barrier(jnp.sum(model_im, axis=-1))
    radj_re, radj_im = adjoint(diff_re, diff_im)
    gnear_re, gnear_im = mat_product(diff_re[..., None], diff_im[..., None], right_re, right_im)
    gfar_re, gfar_im = mat_product(radj_re[..., None], radj_im[..., None], left_re, left_im)
    stacked = jnp.stack((diff_re, diff_im), axis=2)
    resid_block = jnp.transpose(stacked, (4, 0, 1, 2, 3)).reshape(frequency_number, 8, entries_in_tile)
    return (resid_block, from_matrix(-gnear_re, -gnear_im), from_matrix(-gfar_re, -gfar_im))

def reference(pair_uvw_coordinates, directions, brightness, observed, coefficients, station_pair):
    powers, freq_ratio = powers_of(CHANNEL_TOTAL, NP)
    jones_all = evaluate(coefficients, powers)
    entries_in_tile = math.gcd(ANTENNA_PAIRS, 256)
    rotation_number = ANTENNA_PAIRS // entries_in_tile

    def visit_block(running, block_idx):
        begin = (block_idx * entries_in_tile).astype(jnp.int32)
        pick_near = lax.dynamic_slice_in_dim(station_pair[0], begin, entries_in_tile)
        pick_far = lax.dynamic_slice_in_dim(station_pair[1], begin, entries_in_tile)
        coords = lax.dynamic_slice_in_dim(pair_uvw_coordinates, begin, entries_in_tile, 1)
        seen_block = lax.dynamic_slice_in_dim(observed, begin, entries_in_tile, 2)
        resid_block, slope_first_antenna, slope_second_antenna = baseline_terms(jnp.take(jones_all, pick_near, axis=0), jnp.take(jones_all, pick_far, axis=0), coords, directions, brightness, seen_block, freq_ratio)
        running = running + jax.ops.segment_sum(slope_first_antenna, pick_near, num_segments=NS)
        running = running + jax.ops.segment_sum(slope_second_antenna, pick_far, num_segments=NS)
        return (running, resid_block)
    start_sum = jnp.zeros((NS, CHANNEL_TOTAL, 8, K), jnp.float32)
    running, residual_blocks = lax.scan(visit_block, start_sum, jnp.arange(rotation_number, dtype=jnp.int32))
    residual = jnp.transpose(residual_blocks, (1, 2, 0, 3)).reshape(CHANNEL_TOTAL, 8, ANTENNA_PAIRS)
    gradient = contract(running, powers)
    return (gradient, residual)
```

```python
import functools
import math

import jax
import jax.numpy as jnp
from jax import lax
from jax.experimental import pallas as pl
from jax.experimental.pallas import tpu as pltpu
from jax.sharding import PartitionSpec as P

MESH = pl.DeviceIdType.MESH
LANES = 128
ROWS = 8
VMEM_BUDGET = 44 * 1024 * 1024


def powers_of(frequency_number, degree_count):
    channel_pos = jnp.arange(frequency_number, dtype=jnp.float32)
    centre = (2.0 * channel_pos - (frequency_number - 1)) / max(frequency_number - 1, 1)
    levels = [jnp.ones_like(centre)]
    for degree in range(1, degree_count):
        levels.append(levels[-1] * centre)
    return (jnp.stack(levels), 1.0 + 0.25 * centre)


def evaluate(coeff_table, powers):
    degree_count = powers.shape[0]
    shaped = coeff_table.reshape(coeff_table.shape[0], degree_count, 8, coeff_table.shape[2])
    result = shaped[:, 0][:, None] * powers[0][None, :, None, None]
    for degree in range(1, degree_count):
        result = result + shaped[:, degree][:, None] * powers[degree][None, :, None, None]
    return result


def contract(grads, powers):
    pieces = [
        jnp.sum(grads * powers[degree][None, :, None, None], axis=1)
        for degree in range(powers.shape[0])
    ]
    stacked = jnp.stack(pieces, axis=1)
    return stacked.reshape(stacked.shape[0], stacked.shape[1] * 8, stacked.shape[3])


def mat_product(left_re, left_im, right_re, right_im):
    first_re = left_re[:, 0:1] * right_re[0:1] - left_im[:, 0:1] * right_im[0:1]
    second_re = left_re[:, 1:2] * right_re[1:2] - left_im[:, 1:2] * right_im[1:2]
    first_im = left_re[:, 0:1] * right_im[0:1] + left_im[:, 0:1] * right_re[0:1]
    second_im = left_re[:, 1:2] * right_im[1:2] + left_im[:, 1:2] * right_re[1:2]
    return (first_re + second_re, first_im + second_im)


def adjoint(matrix_re, matrix_im):
    return (jnp.swapaxes(matrix_re, 0, 1), -jnp.swapaxes(matrix_im, 0, 1))


def to_matrix(jones_rows):
    shaped = jones_rows.reshape(
        jones_rows.shape[0], jones_rows.shape[1], 2, 2, 2, jones_rows.shape[3]
    )
    real_part = jnp.transpose(shaped[:, :, :, :, 0], (2, 3, 0, 1, 4))
    imag_part = jnp.transpose(shaped[:, :, :, :, 1], (2, 3, 0, 1, 4))
    return (real_part, imag_part)


def from_matrix(real_part, imag_part):
    stacked = jnp.stack((real_part, imag_part), axis=2)
    reordered = jnp.transpose(stacked, (3, 4, 0, 1, 2, 5))
    return reordered.reshape(reordered.shape[0], reordered.shape[1], 8, reordered.shape[5])


def baseline_terms(jones_near, jones_far, coords, directions, brightness, observed, freq_ratio):
    frequency_number = brightness.shape[1]
    dir_count = brightness.shape[2]
    entries_in_tile = coords.shape[1]
    depth_term = jnp.sqrt(1.0 - directions[0] * directions[0] - directions[1] * directions[1]) - 1.0
    inner_sum = (
        coords[0][:, None] * directions[0][None, :]
        + coords[1][:, None] * directions[1][None, :]
        + coords[2][:, None] * depth_term[None, :]
    )
    phase_angle = 2.0 * math.pi * freq_ratio[None, :, None] * inner_sum[:, None, :]
    cosine = jnp.cos(phase_angle)
    sine_part = jnp.sin(phase_angle)
    bright = brightness.reshape(2, 2, 2, frequency_number, dir_count)
    bright_re = bright[:, :, 0][:, :, None]
    bright_im = bright[:, :, 1][:, :, None]
    coh_re = bright_re * cosine + bright_im * sine_part
    coh_im = bright_im * cosine - bright_re * sine_part
    near_re, near_im = to_matrix(jones_near)
    far_re, far_im = to_matrix(jones_far)
    left_re, left_im = mat_product(near_re, near_im, coh_re, coh_im)
    fadj_re, fadj_im = adjoint(far_re, far_im)
    model_re, model_im = mat_product(left_re, left_im, fadj_re, fadj_im)
    cadj_re, cadj_im = adjoint(coh_re, coh_im)
    right_re, right_im = mat_product(far_re, far_im, cadj_re, cadj_im)
    seen_block = observed.reshape(frequency_number, 2, 2, 2, entries_in_tile)
    diff_re = jnp.transpose(seen_block[:, :, :, 0], (1, 2, 3, 0)) - jnp.sum(model_re, axis=-1)
    diff_im = jnp.transpose(seen_block[:, :, :, 1], (1, 2, 3, 0)) - jnp.sum(model_im, axis=-1)
    radj_re, radj_im = adjoint(diff_re, diff_im)
    gnear_re, gnear_im = mat_product(diff_re[..., None], diff_im[..., None], right_re, right_im)
    gfar_re, gfar_im = mat_product(radj_re[..., None], radj_im[..., None], left_re, left_im)
    stacked = jnp.stack((diff_re, diff_im), axis=2)
    resid_block = jnp.transpose(stacked, (4, 0, 1, 2, 3)).reshape(
        frequency_number, 8, entries_in_tile
    )
    return (resid_block, from_matrix(-gnear_re, -gnear_im), from_matrix(-gfar_re, -gfar_im))


def segment_rows(values, stations, row_count):
    inside = (stations >= 0) & (stations < row_count)
    target = jnp.where(inside, stations, row_count)
    return jax.ops.segment_sum(values, target, num_segments=row_count + 1)[:row_count]


def general_shards(pair_uvw_coordinates, directions, brightness, observed, coefficients, station_pair):
    frequency_number = brightness.shape[1]
    dir_count = brightness.shape[2]
    degree_count = coefficients.shape[1] // 8
    stations_dev = coefficients.shape[0]
    pairs_held_here = pair_uvw_coordinates.shape[1]
    powers, freq_ratio = powers_of(frequency_number, degree_count)
    jones_all = evaluate(lax.all_gather(coefficients, "stn", axis=0, tiled=True), powers)
    entries_in_tile = math.gcd(pairs_held_here, 32)
    rotation_number = pairs_held_here // entries_in_tile
    coords_blocks = jnp.transpose(
        pair_uvw_coordinates.reshape(3, rotation_number, entries_in_tile), (1, 0, 2)
    )
    seen_blocks = jnp.transpose(
        observed.reshape(frequency_number, 8, rotation_number, entries_in_tile), (2, 0, 1, 3)
    )
    near_blocks = station_pair[0].reshape(rotation_number, entries_in_tile)
    far_blocks = station_pair[1].reshape(rotation_number, entries_in_tile)

    def visit_block(pieces):
        coords, seen_block, pick_near, pick_far = pieces
        resid_block, slope_first_antenna, slope_second_antenna = baseline_terms(
            jnp.take(jones_all, pick_near, axis=0),
            jnp.take(jones_all, pick_far, axis=0),
            coords,
            directions,
            brightness,
            seen_block,
            freq_ratio,
        )
        slope_first_antenna = contract(slope_first_antenna, powers)
        slope_second_antenna = contract(slope_second_antenna, powers)
        return (
            resid_block,
            slope_first_antenna.reshape(entries_in_tile, -1),
            slope_second_antenna.reshape(entries_in_tile, -1),
        )

    residual_blocks, slope_first_antenna, slope_second_antenna = lax.map(
        visit_block, (coords_blocks, seen_blocks, near_blocks, far_blocks)
    )
    slope_first_antenna = slope_first_antenna.reshape(pairs_held_here, slope_first_antenna.shape[2])
    slope_second_antenna = slope_second_antenna.reshape(
        pairs_held_here, slope_second_antenna.shape[2]
    )
    summed = lax.psum_scatter(
        segment_rows(slope_first_antenna, station_pair[0], lax.axis_size("stn") * stations_dev)
        + segment_rows(slope_second_antenna, station_pair[1], lax.axis_size("stn") * stations_dev),
        "stn",
        scatter_dimension=0,
        tiled=True,
    )
    gradient = summed.reshape(stations_dev, degree_count * 8, dir_count)
    residual = jnp.transpose(residual_blocks, (1, 2, 0, 3)).reshape(
        frequency_number, 8, pairs_held_here
    )
    return (gradient, residual)


def greet(n):
    me = lax.axis_index("stn")
    barrier = pltpu.get_barrier_semaphore()
    for d in range(1, n):
        pl.semaphore_signal(
            barrier, inc=1, device_id={"stn": lax.rem(me + d, n)}, device_id_type=MESH
        )
    pl.semaphore_wait(barrier, n - 1)
    return me


def gather_kernel(n, own_ref, all_ref, send_sem, recv_sem):
    me = greet(n)
    copies = []
    for d in range(1, n):
        copy = pltpu.make_async_remote_copy(
            src_ref=own_ref,
            dst_ref=all_ref.at[me],
            send_sem=send_sem.at[d],
            recv_sem=recv_sem.at[d],
            device_id={"stn": lax.rem(me + d, n)},
            device_id_type=MESH,
        )
        copy.start()
        copies.append(copy)
    all_ref[me] = own_ref[...]
    for copy in copies:
        copy.wait()


def scatter_sum_kernel(n, part_ref, sum_ref, held, send_sem, recv_sem):
    me = greet(n)
    copies = []
    for d in range(1, n):
        peer = lax.rem(me + d, n)
        copy = pltpu.make_async_remote_copy(
            src_ref=part_ref.at[peer],
            dst_ref=held.at[d],
            send_sem=send_sem.at[d],
            recv_sem=recv_sem.at[d],
            device_id={"stn": peer},
            device_id_type=MESH,
        )
        copy.start()
        copies.append(copy)
    total = part_ref[me]
    for d, copy in enumerate(copies, 1):
        copy.wait_recv()
        total = total + held[d]
    sum_ref[...] = total
    for copy in copies:
        copy.wait_send()


def turn_sin_cos(turns):
    x = math.pi * (turns - jnp.round(turns))
    y = x * x
    s = jnp.full_like(y, -1.0 / math.factorial(11))
    for k in (9, 7, 5, 3, 1):
        s = s * y + (1.0 if k % 4 == 1 else -1.0) / math.factorial(k)
    s = s * x
    c = jnp.full_like(y, 1.0 / math.factorial(12))
    for k in (10, 8, 6, 4, 2, 0):
        c = c * y + (1.0 if k % 4 == 0 else -1.0) / math.factorial(k)
    return 2.0 * (s * c), 1.0 - 2.0 * (s * s)


def times(left, right):
    out = []
    for i in range(2):
        for j in range(2):
            (ar, ai), (br, bi) = left[2 * i], right[j]
            (cr, ci), (dr, di) = left[2 * i + 1], right[2 + j]
            out.append(
                (
                    (ar * br - ai * bi) + (cr * dr - ci * di),
                    (ar * bi + ai * br) + (cr * di + ci * dr),
                )
            )
    return out


def times_adj(left, right):
    out = []
    for i in range(2):
        for j in range(2):
            (ar, ai), (br, bi) = left[2 * i], right[2 * j]
            (cr, ci), (dr, di) = left[2 * i + 1], right[2 * j + 1]
            out.append(
                (
                    (ar * br + ai * bi) + (cr * dr + ci * di),
                    (ai * br - ar * bi) + (ci * dr - cr * di),
                )
            )
    return out


def adj_times(left, right):
    out = []
    for i in range(2):
        for j in range(2):
            (ar, ai), (br, bi) = left[i], right[j]
            (cr, ci), (dr, di) = left[2 + i], right[2 + j]
            out.append(
                (
                    (ar * br + ai * bi) + (cr * dr + ci * di),
                    (ar * bi - ai * br) + (cr * di - ci * dr),
                )
            )
    return out


def scaled(er, ei, m):
    return [(er * r - ei * i, er * i + ei * r) for r, i in m]


def scaled_conj(er, ei, m):
    return [(er * r + ei * i, er * i - ei * r) for r, i in m]


def local_kernel(
    degree_count,
    together,
    uvw_ref,
    pair_ref,
    dir_ref,
    bright_ref,
    seen_ref,
    coeff_ref,
    part_ref,
    resid_ref,
    jones,
    with_b,
    with_badj,
    grads,
    seen,
    diffs,
):
    channels = bright_ref.shape[1]
    stations = coeff_ref.shape[0]
    pairs = uvw_ref.shape[1]
    groups = channels // ROWS
    tile = (ROWS, LANES)
    f32 = jnp.float32
    row = lax.broadcasted_iota(jnp.int32, tile, 0)
    lane = lax.broadcasted_iota(jnp.int32, tile, 1)
    span = max(channels - 1, 1)
    xs = [(2.0 * (row + ROWS * g).astype(f32) - (channels - 1)) / span for g in range(groups)]
    ratio = 1.0 + 0.25 * xs[0]
    stride = 0.25 * 2.0 * ROWS / span

    def block(ref, g, lead=()):
        return [
            tuple(
                ref[(*lead, 2 * e + t, pl.ds(ROWS * g, ROWS), slice(None))] for t in range(2)
            )
            for e in range(4)
        ]

    for g in range(groups):
        for comp in range(8):
            seen[comp, pl.ds(ROWS * g, ROWS), :] = seen_ref[
                pl.ds(8 * ROWS * g + comp, ROWS, stride=8), :
            ]

    def prepare(s, carry):
        table = [
            jnp.broadcast_to(coeff_ref[s, pl.ds(i, 1), :], tile) for i in range(8 * degree_count)
        ]
        for g in range(groups):
            rows = pl.ds(ROWS * g, ROWS)
            flat = []
            for comp in range(8):
                value = table[8 * (degree_count - 1) + comp]
                for n in range(degree_count - 2, -1, -1):
                    value = value * xs[g] + table[8 * n + comp]
                flat.append(value)
            j = [(flat[2 * e], flat[2 * e + 1]) for e in range(4)]
            b = block(bright_ref, g)
            a = times(j, b)
            d = times_adj(j, b)
            for e in range(4):
                for t in range(2):
                    jones[s, 2 * e + t, rows, :] = j[e][t]
                    with_b[s, 2 * e + t, rows, :] = a[e][t]
                    with_badj[s, 2 * e + t, rows, :] = d[e][t]
                    grads[s, 2 * e + t, rows, :] = jnp.zeros(tile, f32)
        return carry

    lax.fori_loop(0, stations, prepare, 0)

    l = jnp.broadcast_to(dir_ref[0:1, :], tile)
    m = jnp.broadcast_to(dir_ref[1:2, :], tile)
    depth = jnp.sqrt(1.0 - l * l - m * m) - 1.0

    def predict(b):
        p, q = pair_ref[0, b], pair_ref[1, b]
        inner = uvw_ref[0, b] * l + uvw_ref[1, b] * m + uvw_ref[2, b] * depth
        s, c = turn_sin_cos(ratio * inner)
        step_s, step_c = turn_sin_cos(stride * inner)
        er, ei = c, -s
        here = lane == b
        out = []
        for g in range(groups):
            if g:
                er, ei = er * step_c + ei * step_s, ei * step_c - er * step_s
            t = scaled(er, ei, block(with_b, g, (p,)))
            model = times_adj(t, block(jones, g, (q,)))
            rows = pl.ds(ROWS * g, ROWS)
            diff = []
            for e in range(4):
                pieces = []
                for k in range(2):
                    comp = 2 * e + k
                    term = model[e][k] - jnp.where(here, seen[comp, rows, :], 0.0)
                    total = jnp.broadcast_to(jnp.sum(term, axis=1, keepdims=True), tile)
                    pltpu.store(diffs.at[comp, rows, :], total, mask=here)
                    pieces.append(total)
                diff.append(tuple(pieces))
            out.append((er, ei, t, diff))
        return p, q, out

    def deposit(state):
        p, q, out = state
        for g in range(groups):
            rows = pl.ds(ROWS * g, ROWS)
            er, ei, t, diff = out[g]
            near = times(diff, scaled_conj(er, ei, block(with_badj, g, (q,))))
            far = adj_times(diff, t)
            for station, slope in ((p, near), (q, far)):
                for e in range(4):
                    for k in range(2):
                        grads[station, 2 * e + k, rows, :] += slope[e][k]

    def visit(i, carry):
        last = predict(i * together)
        for u in range(1, together):
            state = predict(i * together + u)
            deposit(last)
            last = state
        deposit(last)
        return carry

    lax.fori_loop(0, pairs // together, visit, 0)

    def finish(s, carry):
        for comp in range(8):
            terms = [grads[s, comp, pl.ds(ROWS * g, ROWS), :] for g in range(groups)]
            for n in range(degree_count):
                if n:
                    terms = [v * x for v, x in zip(terms, xs)]
                part_ref[s, pl.ds(8 * n + comp, 1), :] = jnp.sum(
                    sum(terms[1:], terms[0]), axis=0, keepdims=True
                )
        return carry

    lax.fori_loop(0, stations, finish, 0)

    for g in range(groups):
        for comp in range(8):
            resid_ref[pl.ds(8 * ROWS * g + comp, ROWS, stride=8), :] = -diffs[
                comp, pl.ds(ROWS * g, ROWS), :
            ]


def gather(own, n):
    vmem = pl.BlockSpec(memory_space=pltpu.VMEM)
    return pl.pallas_call(
        functools.partial(gather_kernel, n),
        out_shape=jax.ShapeDtypeStruct((n, *own.shape), own.dtype),
        in_specs=[vmem],
        out_specs=vmem,
        scratch_shapes=[pltpu.SemaphoreType.DMA((n,)), pltpu.SemaphoreType.DMA((n,))],
        compiler_params=pltpu.CompilerParams(collective_id=1, has_side_effects=True),
        name="gather_coefficients",
    )(own)


def scatter_sum(parts, n):
    vmem = pl.BlockSpec(memory_space=pltpu.VMEM)
    return pl.pallas_call(
        functools.partial(scatter_sum_kernel, n),
        out_shape=jax.ShapeDtypeStruct(parts.shape[1:], parts.dtype),
        in_specs=[vmem],
        out_specs=vmem,
        scratch_shapes=[
            pltpu.VMEM(parts.shape, parts.dtype),
            pltpu.SemaphoreType.DMA((n,)),
            pltpu.SemaphoreType.DMA((n,)),
        ],
        compiler_params=pltpu.CompilerParams(collective_id=2, has_side_effects=True),
        name="sum_gradient",
    )(parts)


def compact_shards(uvw, directions, brightness, observed, coefficients, pair):
    n = lax.axis_size("stn")
    channels, dirs = brightness.shape[1:]
    held, rows = coefficients.shape[:2]
    pairs = uvw.shape[1]
    table = gather(coefficients, n).reshape(n * held, rows, dirs)
    vmem = pl.BlockSpec(memory_space=pltpu.VMEM)
    smem = pl.BlockSpec(memory_space=pltpu.SMEM)
    per_station = pltpu.VMEM((n * held, 8, channels, dirs), jnp.float32)
    per_pair = pltpu.VMEM((8, channels, pairs), jnp.float32)
    partial, residual = pl.pallas_call(
        functools.partial(local_kernel, rows // 8, 4),
        out_shape=(
            jax.ShapeDtypeStruct(table.shape, jnp.float32),
            jax.ShapeDtypeStruct((channels * 8, pairs), jnp.float32),
        ),
        in_specs=[smem, smem, vmem, vmem, vmem, vmem],
        out_specs=(vmem, vmem),
        scratch_shapes=[per_station] * 4 + [per_pair] * 2,
        compiler_params=pltpu.CompilerParams(vmem_limit_bytes=VMEM_BUDGET),
        name="predict_and_slope",
    )(uvw, pair, directions, brightness, observed.reshape(channels * 8, pairs), table)
    gradient = scatter_sum(partial.reshape(n, held, rows, dirs), n)
    return gradient, residual.reshape(channels, 8, pairs)


def shards(uvw, directions, brightness, observed, coefficients, pair):
    channels, dirs = brightness.shape[1:]
    stations = lax.axis_size("stn") * coefficients.shape[0]
    fits = 4 * stations * 8 * channels * dirs * 4 <= VMEM_BUDGET // 2
    if fits and dirs == LANES and uvw.shape[1] == LANES and channels % ROWS == 0:
        return compact_shards(uvw, directions, brightness, observed, coefficients, pair)
    return general_shards(uvw, directions, brightness, observed, coefficients, pair)


def solution(mesh):
    placed = (
        P(None, ("grp", "stn")),
        P(),
        P(),
        P(None, None, ("grp", "stn")),
        P(("grp", "stn"), None, None),
        P(None, ("grp", "stn")),
    )
    return jax.shard_map(
        shards,
        mesh=mesh,
        in_specs=placed,
        out_specs=(P(("grp", "stn"), None, None), P(None, None, ("grp", "stn"))),
        check_vma=False,
    )
```

```python
import functools
import math

import jax
import jax.numpy as jnp
from jax import lax
from jax.experimental import pallas as pl
from jax.experimental.pallas import tpu as pltpu
from jax.sharding import PartitionSpec as P

MESH = pl.DeviceIdType.MESH
LANES = 128
ROWS = 8
VMEM_BUDGET = 44 * 1024 * 1024


def powers_of(frequency_number, degree_count):
    channel_pos = jnp.arange(frequency_number, dtype=jnp.float32)
    centre = (2.0 * channel_pos - (frequency_number - 1)) / max(frequency_number - 1, 1)
    levels = [jnp.ones_like(centre)]
    for degree in range(1, degree_count):
        levels.append(levels[-1] * centre)
    return (jnp.stack(levels), 1.0 + 0.25 * centre)


def evaluate(coeff_table, powers):
    degree_count = powers.shape[0]
    shaped = coeff_table.reshape(coeff_table.shape[0], degree_count, 8, coeff_table.shape[2])
    result = shaped[:, 0][:, None] * powers[0][None, :, None, None]
    for degree in range(1, degree_count):
        result = result + shaped[:, degree][:, None] * powers[degree][None, :, None, None]
    return result


def contract(grads, powers):
    pieces = [
        jnp.sum(grads * powers[degree][None, :, None, None], axis=1)
        for degree in range(powers.shape[0])
    ]
    stacked = jnp.stack(pieces, axis=1)
    return stacked.reshape(stacked.shape[0], stacked.shape[1] * 8, stacked.shape[3])


def mat_product(left_re, left_im, right_re, right_im):
    first_re = left_re[:, 0:1] * right_re[0:1] - left_im[:, 0:1] * right_im[0:1]
    second_re = left_re[:, 1:2] * right_re[1:2] - left_im[:, 1:2] * right_im[1:2]
    first_im = left_re[:, 0:1] * right_im[0:1] + left_im[:, 0:1] * right_re[0:1]
    second_im = left_re[:, 1:2] * right_im[1:2] + left_im[:, 1:2] * right_re[1:2]
    return (first_re + second_re, first_im + second_im)


def adjoint(matrix_re, matrix_im):
    return (jnp.swapaxes(matrix_re, 0, 1), -jnp.swapaxes(matrix_im, 0, 1))


def to_matrix(jones_rows):
    shaped = jones_rows.reshape(
        jones_rows.shape[0], jones_rows.shape[1], 2, 2, 2, jones_rows.shape[3]
    )
    real_part = jnp.transpose(shaped[:, :, :, :, 0], (2, 3, 0, 1, 4))
    imag_part = jnp.transpose(shaped[:, :, :, :, 1], (2, 3, 0, 1, 4))
    return (real_part, imag_part)


def from_matrix(real_part, imag_part):
    stacked = jnp.stack((real_part, imag_part), axis=2)
    reordered = jnp.transpose(stacked, (3, 4, 0, 1, 2, 5))
    return reordered.reshape(reordered.shape[0], reordered.shape[1], 8, reordered.shape[5])


def baseline_terms(jones_near, jones_far, coords, directions, brightness, observed, freq_ratio):
    frequency_number = brightness.shape[1]
    dir_count = brightness.shape[2]
    entries_in_tile = coords.shape[1]
    depth_term = jnp.sqrt(1.0 - directions[0] * directions[0] - directions[1] * directions[1]) - 1.0
    inner_sum = (
        coords[0][:, None] * directions[0][None, :]
        + coords[1][:, None] * directions[1][None, :]
        + coords[2][:, None] * depth_term[None, :]
    )
    phase_angle = 2.0 * math.pi * freq_ratio[None, :, None] * inner_sum[:, None, :]
    cosine = jnp.cos(phase_angle)
    sine_part = jnp.sin(phase_angle)
    bright = brightness.reshape(2, 2, 2, frequency_number, dir_count)
    bright_re = bright[:, :, 0][:, :, None]
    bright_im = bright[:, :, 1][:, :, None]
    coh_re = bright_re * cosine + bright_im * sine_part
    coh_im = bright_im * cosine - bright_re * sine_part
    near_re, near_im = to_matrix(jones_near)
    far_re, far_im = to_matrix(jones_far)
    left_re, left_im = mat_product(near_re, near_im, coh_re, coh_im)
    fadj_re, fadj_im = adjoint(far_re, far_im)
    model_re, model_im = mat_product(left_re, left_im, fadj_re, fadj_im)
    cadj_re, cadj_im = adjoint(coh_re, coh_im)
    right_re, right_im = mat_product(far_re, far_im, cadj_re, cadj_im)
    seen_block = observed.reshape(frequency_number, 2, 2, 2, entries_in_tile)
    diff_re = jnp.transpose(seen_block[:, :, :, 0], (1, 2, 3, 0)) - jnp.sum(model_re, axis=-1)
    diff_im = jnp.transpose(seen_block[:, :, :, 1], (1, 2, 3, 0)) - jnp.sum(model_im, axis=-1)
    radj_re, radj_im = adjoint(diff_re, diff_im)
    gnear_re, gnear_im = mat_product(diff_re[..., None], diff_im[..., None], right_re, right_im)
    gfar_re, gfar_im = mat_product(radj_re[..., None], radj_im[..., None], left_re, left_im)
    stacked = jnp.stack((diff_re, diff_im), axis=2)
    resid_block = jnp.transpose(stacked, (4, 0, 1, 2, 3)).reshape(
        frequency_number, 8, entries_in_tile
    )
    return (resid_block, from_matrix(-gnear_re, -gnear_im), from_matrix(-gfar_re, -gfar_im))


def segment_rows(values, stations, row_count):
    inside = (stations >= 0) & (stations < row_count)
    target = jnp.where(inside, stations, row_count)
    return jax.ops.segment_sum(values, target, num_segments=row_count + 1)[:row_count]


def general_shards(pair_uvw_coordinates, directions, brightness, observed, coefficients, station_pair):
    frequency_number = brightness.shape[1]
    dir_count = brightness.shape[2]
    degree_count = coefficients.shape[1] // 8
    stations_dev = coefficients.shape[0]
    pairs_held_here = pair_uvw_coordinates.shape[1]
    powers, freq_ratio = powers_of(frequency_number, degree_count)
    jones_all = evaluate(lax.all_gather(coefficients, "stn", axis=0, tiled=True), powers)
    entries_in_tile = math.gcd(pairs_held_here, 32)
    rotation_number = pairs_held_here // entries_in_tile
    coords_blocks = jnp.transpose(
        pair_uvw_coordinates.reshape(3, rotation_number, entries_in_tile), (1, 0, 2)
    )
    seen_blocks = jnp.transpose(
        observed.reshape(frequency_number, 8, rotation_number, entries_in_tile), (2, 0, 1, 3)
    )
    near_blocks = station_pair[0].reshape(rotation_number, entries_in_tile)
    far_blocks = station_pair[1].reshape(rotation_number, entries_in_tile)

    def visit_block(pieces):
        coords, seen_block, pick_near, pick_far = pieces
        resid_block, slope_first_antenna, slope_second_antenna = baseline_terms(
            jnp.take(jones_all, pick_near, axis=0),
            jnp.take(jones_all, pick_far, axis=0),
            coords,
            directions,
            brightness,
            seen_block,
            freq_ratio,
        )
        slope_first_antenna = contract(slope_first_antenna, powers)
        slope_second_antenna = contract(slope_second_antenna, powers)
        return (
            resid_block,
            slope_first_antenna.reshape(entries_in_tile, -1),
            slope_second_antenna.reshape(entries_in_tile, -1),
        )

    residual_blocks, slope_first_antenna, slope_second_antenna = lax.map(
        visit_block, (coords_blocks, seen_blocks, near_blocks, far_blocks)
    )
    slope_first_antenna = slope_first_antenna.reshape(pairs_held_here, slope_first_antenna.shape[2])
    slope_second_antenna = slope_second_antenna.reshape(
        pairs_held_here, slope_second_antenna.shape[2]
    )
    summed = lax.psum_scatter(
        segment_rows(slope_first_antenna, station_pair[0], lax.axis_size("stn") * stations_dev)
        + segment_rows(slope_second_antenna, station_pair[1], lax.axis_size("stn") * stations_dev),
        "stn",
        scatter_dimension=0,
        tiled=True,
    )
    gradient = summed.reshape(stations_dev, degree_count * 8, dir_count)
    residual = jnp.transpose(residual_blocks, (1, 2, 0, 3)).reshape(
        frequency_number, 8, pairs_held_here
    )
    return (gradient, residual)


def place(n):
    cores = 2 if n % 2 == 0 else 1
    columns = 2 if n % (2 * cores) == 0 else 1
    depth = n // (cores * columns)
    me = lax.axis_index("stn")
    z, rest = lax.div(me, cores * columns), lax.rem(me, cores * columns)
    return depth, columns, cores, z, lax.div(rest, cores), lax.rem(rest, cores)


class Hops:
    def __init__(self, n, send_sem, recv_sem):
        self.depth, self.columns, self.cores, self.z, self.x, self.c = place(n)
        self.send_sem, self.recv_sem = send_sem, recv_sem
        self.copies = {}

    def index(self, dz, dx, dc):
        z = lax.rem(self.z + dz + self.depth, self.depth)
        x = 1 - self.x if dx else self.x
        c = 1 - self.c if dc else self.c
        return (z * self.columns + x) * self.cores + c

    def greet(self):
        barrier = pltpu.get_barrier_semaphore()
        peers = [(d, 0, 0) for d in range(1, self.depth)]
        peers += [(0, 1, 0)] * (self.columns > 1) + [(0, 0, 1)] * (self.cores > 1)
        for peer in peers:
            pl.semaphore_signal(
                barrier, inc=1, device_id={"stn": self.index(*peer)}, device_id_type=MESH
            )
        pl.semaphore_wait(barrier, len(peers))

    def send(self, key, peer, src, dst):
        number = len(self.copies)
        copy = pltpu.make_async_remote_copy(
            src_ref=src,
            dst_ref=dst,
            send_sem=self.send_sem.at[number],
            recv_sem=self.recv_sem.at[number],
            device_id={"stn": self.index(*peer)},
            device_id_type=MESH,
        )
        copy.start()
        self.copies[key] = copy

    def arrived(self, key):
        self.copies[key].wait_recv()

    def settle(self):
        for copy in self.copies.values():
            copy.wait_send()


def gather_kernel(n, own_ref, all_ref, held, send_sem, recv_sem, out_sem):
    hops = Hops(n, send_sem, recv_sem)
    outs = []

    def keep(src, slot):
        out = pltpu.make_async_copy(src, all_ref.at[slot], out_sem.at[len(outs)])
        out.start()
        outs.append(out)

    me = hops.index(0, 0, 0)
    mine = held.at[me]
    hops.greet()
    for d in range(1, hops.depth):
        hops.send(("z", d), (d, 0, 0), own_ref, mine)
    hops.send(("x", 0), (0, 1, 0), own_ref, mine)
    hops.send(("c", 0, 0), (0, 0, 1), own_ref, mine)
    keep(own_ref, me)
    for d in range(1, hops.depth):
        hops.arrived(("z", d))
        slot = hops.index(-d, 0, 0)
        hops.send(("x", d), (0, 1, 0), held.at[slot], held.at[slot])
        hops.send(("c", d, 0), (0, 0, 1), held.at[slot], held.at[slot])
        keep(held.at[slot], slot)
    for d in range(hops.depth):
        hops.arrived(("x", d))
        slot = hops.index(-d, 1, 0)
        hops.send(("c", d, 1), (0, 0, 1), held.at[slot], held.at[slot])
        keep(held.at[slot], slot)
    for dx in range(2):
        for d in range(hops.depth):
            hops.arrived(("c", d, dx))
            slot = hops.index(-d, dx, 1)
            keep(held.at[slot], slot)
    for out in outs:
        out.wait()
    hops.settle()


def scatter_sum_kernel(n, part_ref, sum_ref, own, from_c, from_x, from_z, send_sem, recv_sem, in_sem):
    hops = Hops(n, send_sem, recv_sem)
    order = [(d, dx) for dx in (1, 0) for d in [*range(1, hops.depth), 0]]
    ins = {}
    for k, (d, dx) in enumerate(order):
        ins[d, dx] = pltpu.make_async_copy(
            part_ref.at[hops.index(d, dx, 0)], own.at[dx, d], in_sem.at[k]
        )
        ins[d, dx].start()
    hops.greet()
    for d, dx in order:
        hops.send(
            ("c", d, dx), (0, 0, 1), part_ref.at[hops.index(d, dx, 1)], from_c.at[dx, d]
        )
    for d, dx in order:
        ins[d, dx].wait()
        hops.arrived(("c", d, dx))
        if dx:
            own[dx, d] = own[dx, d] + from_c[dx, d]
            hops.send(("x", d), (0, 1, 0), own.at[dx, d], from_x.at[d])
            continue
        hops.arrived(("x", d))
        total = own[dx, d] + from_c[dx, d] + from_x[d]
        if d:
            own[dx, d] = total
            hops.send(("z", d), (d, 0, 0), own.at[dx, d], from_z.at[d])
    for d in range(1, hops.depth):
        hops.arrived(("z", d))
        total = total + from_z[d]
    sum_ref[...] = total
    hops.settle()


def turn_sin_cos(turns):
    x = math.pi * (turns - jnp.round(turns))
    y = x * x
    s = jnp.full_like(y, -1.0 / math.factorial(11))
    for k in (9, 7, 5, 3, 1):
        s = s * y + (1.0 if k % 4 == 1 else -1.0) / math.factorial(k)
    s = s * x
    c = jnp.full_like(y, 1.0 / math.factorial(12))
    for k in (10, 8, 6, 4, 2, 0):
        c = c * y + (1.0 if k % 4 == 0 else -1.0) / math.factorial(k)
    return 2.0 * (s * c), 1.0 - 2.0 * (s * s)


def times(left, right):
    out = []
    for i in range(2):
        for j in range(2):
            (ar, ai), (br, bi) = left[2 * i], right[j]
            (cr, ci), (dr, di) = left[2 * i + 1], right[2 + j]
            out.append(
                (
                    (ar * br - ai * bi) + (cr * dr - ci * di),
                    (ar * bi + ai * br) + (cr * di + ci * dr),
                )
            )
    return out


def times_adj(left, right):
    out = []
    for i in range(2):
        for j in range(2):
            (ar, ai), (br, bi) = left[2 * i], right[2 * j]
            (cr, ci), (dr, di) = left[2 * i + 1], right[2 * j + 1]
            out.append(
                (
                    (ar * br + ai * bi) + (cr * dr + ci * di),
                    (ai * br - ar * bi) + (ci * dr - cr * di),
                )
            )
    return out


def adj_times(left, right):
    out = []
    for i in range(2):
        for j in range(2):
            (ar, ai), (br, bi) = left[i], right[j]
            (cr, ci), (dr, di) = left[2 + i], right[2 + j]
            out.append(
                (
                    (ar * br + ai * bi) + (cr * dr + ci * di),
                    (ar * bi - ai * br) + (cr * di - ci * dr),
                )
            )
    return out


def scaled(er, ei, m):
    return [(er * r - ei * i, er * i + ei * r) for r, i in m]


def scaled_conj(er, ei, m):
    return [(er * r + ei * i, er * i - ei * r) for r, i in m]


def local_kernel(
    degree_count,
    together,
    uvw_ref,
    pair_hbm,
    dir_ref,
    bright_ref,
    seen_ref,
    coeff_hbm,
    part_hbm,
    resid_ref,
    pair_ref,
    coeff_ref,
    part_ref,
    jones,
    with_b,
    with_badj,
    grads,
    seen,
    diffs,
    pair_sem,
    table_sem,
):
    channels = bright_ref.shape[1]
    stations = coeff_ref.shape[0]
    chunk = stations // table_sem.shape[0]

    def span_of(s):
        return pl.ds(pl.multiple_of(lax.div(s, chunk) * chunk, chunk), chunk)

    def table_in(s):
        return pltpu.make_async_copy(
            coeff_hbm.at[span_of(s)], coeff_ref.at[span_of(s)], table_sem.at[lax.div(s, chunk)]
        )

    def part_out(s):
        return pltpu.make_async_copy(
            part_ref.at[span_of(s)], part_hbm.at[span_of(s)], table_sem.at[lax.div(s, chunk)]
        )

    for k in range(table_sem.shape[0]):
        table_in(k * chunk).start()
    pair_in = pltpu.make_async_copy(pair_hbm, pair_ref, pair_sem)
    pair_in.start()
    pairs = uvw_ref.shape[1]
    groups = channels // ROWS
    tile = (ROWS, LANES)
    f32 = jnp.float32
    row = lax.broadcasted_iota(jnp.int32, tile, 0)
    lane = lax.broadcasted_iota(jnp.int32, tile, 1)
    span = max(channels - 1, 1)
    xs = [(2.0 * (row + ROWS * g).astype(f32) - (channels - 1)) / span for g in range(groups)]
    ratio = 1.0 + 0.25 * xs[0]
    stride = 0.25 * 2.0 * ROWS / span

    def block(ref, g, lead=()):
        return [
            tuple(
                ref[(*lead, 2 * e + t, pl.ds(ROWS * g, ROWS), slice(None))] for t in range(2)
            )
            for e in range(4)
        ]

    for g in range(groups):
        for comp in range(8):
            seen[comp, pl.ds(ROWS * g, ROWS), :] = seen_ref[
                pl.ds(8 * ROWS * g + comp, ROWS, stride=8), :
            ]

    def prepare(s, carry):
        @pl.when(lax.rem(s, chunk) == 0)
        def _():
            table_in(s).wait()

        table = [
            jnp.broadcast_to(coeff_ref[s, pl.ds(i, 1), :], tile) for i in range(8 * degree_count)
        ]
        for g in range(groups):
            rows = pl.ds(ROWS * g, ROWS)
            flat = []
            for comp in range(8):
                value = table[8 * (degree_count - 1) + comp]
                for n in range(degree_count - 2, -1, -1):
                    value = value * xs[g] + table[8 * n + comp]
                flat.append(value)
            j = [(flat[2 * e], flat[2 * e + 1]) for e in range(4)]
            b = block(bright_ref, g)
            a = times(j, b)
            d = times_adj(j, b)
            for e in range(4):
                for t in range(2):
                    jones[s, 2 * e + t, rows, :] = j[e][t]
                    with_b[s, 2 * e + t, rows, :] = a[e][t]
                    with_badj[s, 2 * e + t, rows, :] = d[e][t]
                    grads[s, 2 * e + t, rows, :] = jnp.zeros(tile, f32)
        return carry

    lax.fori_loop(0, stations, prepare, 0)
    pair_in.wait()

    l = jnp.broadcast_to(dir_ref[0:1, :], tile)
    m = jnp.broadcast_to(dir_ref[1:2, :], tile)
    depth = jnp.sqrt(1.0 - l * l - m * m) - 1.0

    def predict(b):
        p, q = pair_ref[0, b], pair_ref[1, b]
        inner = uvw_ref[0, b] * l + uvw_ref[1, b] * m + uvw_ref[2, b] * depth
        s, c = turn_sin_cos(ratio * inner)
        step_s, step_c = turn_sin_cos(stride * inner)
        er, ei = c, -s
        here = lane == b
        out = []
        for g in range(groups):
            if g:
                er, ei = er * step_c + ei * step_s, ei * step_c - er * step_s
            t = scaled(er, ei, block(with_b, g, (p,)))
            model = times_adj(t, block(jones, g, (q,)))
            rows = pl.ds(ROWS * g, ROWS)
            diff = []
            for e in range(4):
                pieces = []
                for k in range(2):
                    comp = 2 * e + k
                    term = model[e][k] - jnp.where(here, seen[comp, rows, :], 0.0)
                    total = jnp.broadcast_to(jnp.sum(term, axis=1, keepdims=True), tile)
                    pltpu.store(diffs.at[comp, rows, :], total, mask=here)
                    pieces.append(total)
                diff.append(tuple(pieces))
            out.append((er, ei, t, diff))
        return p, q, out

    def deposit(state):
        p, q, out = state
        for g in range(groups):
            rows = pl.ds(ROWS * g, ROWS)
            er, ei, t, diff = out[g]
            near = times(diff, scaled_conj(er, ei, block(with_badj, g, (q,))))
            far = adj_times(diff, t)
            for station, slope in ((p, near), (q, far)):
                for e in range(4):
                    for k in range(2):
                        grads[station, 2 * e + k, rows, :] += slope[e][k]

    def visit(i, carry):
        last = predict(i * together)
        for u in range(1, together):
            state = predict(i * together + u)
            deposit(last)
            last = state
        deposit(last)
        return carry

    lax.fori_loop(0, pairs // together, visit, 0)

    def finish(s, carry):
        for comp in range(8):
            terms = [grads[s, comp, pl.ds(ROWS * g, ROWS), :] for g in range(groups)]
            for n in range(degree_count):
                if n:
                    terms = [v * x for v, x in zip(terms, xs)]
                part_ref[s, pl.ds(8 * n + comp, 1), :] = jnp.sum(
                    sum(terms[1:], terms[0]), axis=0, keepdims=True
                )

        @pl.when(lax.rem(s, chunk) == chunk - 1)
        def _():
            part_out(s).start()

        return carry

    lax.fori_loop(0, stations, finish, 0)

    for g in range(groups):
        for comp in range(8):
            resid_ref[pl.ds(8 * ROWS * g + comp, ROWS, stride=8), :] = -diffs[
                comp, pl.ds(ROWS * g, ROWS), :
            ]
    for k in range(table_sem.shape[0]):
        part_out(k * chunk).wait()


def gather(own, n):
    return pl.pallas_call(
        functools.partial(gather_kernel, n),
        out_shape=jax.ShapeDtypeStruct((n, *own.shape), own.dtype),
        in_specs=[pl.BlockSpec(memory_space=pltpu.VMEM)],
        out_specs=pl.BlockSpec(memory_space=pl.ANY),
        scratch_shapes=[
            pltpu.VMEM((n, *own.shape), own.dtype),
            pltpu.SemaphoreType.DMA((n,)),
            pltpu.SemaphoreType.DMA((n,)),
            pltpu.SemaphoreType.DMA((n,)),
        ],
        compiler_params=pltpu.CompilerParams(collective_id=1, has_side_effects=True),
        name="gather_coefficients",
    )(own)


def scatter_sum(parts, n):
    piece = parts.shape[1:]
    return pl.pallas_call(
        functools.partial(scatter_sum_kernel, n),
        out_shape=jax.ShapeDtypeStruct(piece, parts.dtype),
        in_specs=[pl.BlockSpec(memory_space=pl.ANY)],
        out_specs=pl.BlockSpec(memory_space=pltpu.VMEM),
        scratch_shapes=[
            pltpu.VMEM((2, n // 4, *piece), parts.dtype),
            pltpu.VMEM((2, n // 4, *piece), parts.dtype),
            pltpu.VMEM((n // 4, *piece), parts.dtype),
            pltpu.VMEM((n // 4, *piece), parts.dtype),
            pltpu.SemaphoreType.DMA((n,)),
            pltpu.SemaphoreType.DMA((n,)),
            pltpu.SemaphoreType.DMA((n,)),
        ],
        compiler_params=pltpu.CompilerParams(collective_id=2, has_side_effects=True),
        name="sum_gradient",
    )(parts)


def compact_shards(uvw, directions, brightness, observed, coefficients, pair):
    n = lax.axis_size("stn")
    channels, dirs = brightness.shape[1:]
    held, rows = coefficients.shape[:2]
    pairs = uvw.shape[1]
    table = gather(coefficients, n).reshape(n * held, rows, dirs)
    vmem = pl.BlockSpec(memory_space=pltpu.VMEM)
    away = pl.BlockSpec(memory_space=pl.ANY)
    smem = pl.BlockSpec(memory_space=pltpu.SMEM)
    per_station = pltpu.VMEM((n * held, 8, channels, dirs), jnp.float32)
    per_pair = pltpu.VMEM((8, channels, pairs), jnp.float32)
    partial, residual = pl.pallas_call(
        functools.partial(local_kernel, rows // 8, 4),
        out_shape=(
            jax.ShapeDtypeStruct(table.shape, jnp.float32),
            jax.ShapeDtypeStruct((channels * 8, pairs), jnp.float32),
        ),
        in_specs=[smem, away, vmem, vmem, vmem, away],
        out_specs=(away, vmem),
        scratch_shapes=[pltpu.SMEM(pair.shape, pair.dtype)]
        + [pltpu.VMEM(table.shape, jnp.float32)] * 2
        + [per_station] * 4
        + [per_pair] * 2
        + [pltpu.SemaphoreType.DMA, pltpu.SemaphoreType.DMA((4,))],
        compiler_params=pltpu.CompilerParams(vmem_limit_bytes=VMEM_BUDGET),
        name="predict_and_slope",
    )(uvw, pair, directions, brightness, observed.reshape(channels * 8, pairs), table)
    gradient = scatter_sum(partial.reshape(n, held, rows, dirs), n)
    return gradient, residual.reshape(channels, 8, pairs)


def shards(uvw, directions, brightness, observed, coefficients, pair):
    channels, dirs = brightness.shape[1:]
    stations = lax.axis_size("stn") * coefficients.shape[0]
    fits = lax.axis_size("stn") % 4 == 0 and 4 * stations * 8 * channels * dirs * 4 <= VMEM_BUDGET // 2
    if fits and dirs == LANES and uvw.shape[1] == LANES and channels % ROWS == 0:
        return compact_shards(uvw, directions, brightness, observed, coefficients, pair)
    return general_shards(uvw, directions, brightness, observed, coefficients, pair)


def solution(mesh):
    placed = (
        P(None, ("grp", "stn")),
        P(),
        P(),
        P(None, None, ("grp", "stn")),
        P(("grp", "stn"), None, None),
        P(None, ("grp", "stn")),
    )
    return jax.shard_map(
        shards,
        mesh=mesh,
        in_specs=placed,
        out_specs=(P(("grp", "stn"), None, None), P(None, None, ("grp", "stn"))),
        check_vma=False,
    )
```

```python
import functools
import math

import jax
import jax.numpy as jnp
from jax import lax
from jax.experimental import pallas as pl
from jax.experimental.pallas import tpu as pltpu
from jax.sharding import PartitionSpec as P

MESH = pl.DeviceIdType.MESH
LANES = 128
ROWS = 8
VMEM_BUDGET = 44 * 1024 * 1024


def powers_of(frequency_number, degree_count):
    channel_pos = jnp.arange(frequency_number, dtype=jnp.float32)
    centre = (2.0 * channel_pos - (frequency_number - 1)) / max(frequency_number - 1, 1)
    levels = [jnp.ones_like(centre)]
    for degree in range(1, degree_count):
        levels.append(levels[-1] * centre)
    return (jnp.stack(levels), 1.0 + 0.25 * centre)


def evaluate(coeff_table, powers):
    degree_count = powers.shape[0]
    shaped = coeff_table.reshape(coeff_table.shape[0], degree_count, 8, coeff_table.shape[2])
    result = shaped[:, 0][:, None] * powers[0][None, :, None, None]
    for degree in range(1, degree_count):
        result = result + shaped[:, degree][:, None] * powers[degree][None, :, None, None]
    return result


def contract(grads, powers):
    pieces = [
        jnp.sum(grads * powers[degree][None, :, None, None], axis=1)
        for degree in range(powers.shape[0])
    ]
    stacked = jnp.stack(pieces, axis=1)
    return stacked.reshape(stacked.shape[0], stacked.shape[1] * 8, stacked.shape[3])


def mat_product(left_re, left_im, right_re, right_im):
    first_re = left_re[:, 0:1] * right_re[0:1] - left_im[:, 0:1] * right_im[0:1]
    second_re = left_re[:, 1:2] * right_re[1:2] - left_im[:, 1:2] * right_im[1:2]
    first_im = left_re[:, 0:1] * right_im[0:1] + left_im[:, 0:1] * right_re[0:1]
    second_im = left_re[:, 1:2] * right_im[1:2] + left_im[:, 1:2] * right_re[1:2]
    return (first_re + second_re, first_im + second_im)


def adjoint(matrix_re, matrix_im):
    return (jnp.swapaxes(matrix_re, 0, 1), -jnp.swapaxes(matrix_im, 0, 1))


def to_matrix(jones_rows):
    shaped = jones_rows.reshape(
        jones_rows.shape[0], jones_rows.shape[1], 2, 2, 2, jones_rows.shape[3]
    )
    real_part = jnp.transpose(shaped[:, :, :, :, 0], (2, 3, 0, 1, 4))
    imag_part = jnp.transpose(shaped[:, :, :, :, 1], (2, 3, 0, 1, 4))
    return (real_part, imag_part)


def from_matrix(real_part, imag_part):
    stacked = jnp.stack((real_part, imag_part), axis=2)
    reordered = jnp.transpose(stacked, (3, 4, 0, 1, 2, 5))
    return reordered.reshape(reordered.shape[0], reordered.shape[1], 8, reordered.shape[5])


def baseline_terms(jones_near, jones_far, coords, directions, brightness, observed, freq_ratio):
    frequency_number = brightness.shape[1]
    dir_count = brightness.shape[2]
    entries_in_tile = coords.shape[1]
    depth_term = jnp.sqrt(1.0 - directions[0] * directions[0] - directions[1] * directions[1]) - 1.0
    inner_sum = (
        coords[0][:, None] * directions[0][None, :]
        + coords[1][:, None] * directions[1][None, :]
        + coords[2][:, None] * depth_term[None, :]
    )
    phase_angle = 2.0 * math.pi * freq_ratio[None, :, None] * inner_sum[:, None, :]
    cosine = jnp.cos(phase_angle)
    sine_part = jnp.sin(phase_angle)
    bright = brightness.reshape(2, 2, 2, frequency_number, dir_count)
    bright_re = bright[:, :, 0][:, :, None]
    bright_im = bright[:, :, 1][:, :, None]
    coh_re = bright_re * cosine + bright_im * sine_part
    coh_im = bright_im * cosine - bright_re * sine_part
    near_re, near_im = to_matrix(jones_near)
    far_re, far_im = to_matrix(jones_far)
    left_re, left_im = mat_product(near_re, near_im, coh_re, coh_im)
    fadj_re, fadj_im = adjoint(far_re, far_im)
    model_re, model_im = mat_product(left_re, left_im, fadj_re, fadj_im)
    cadj_re, cadj_im = adjoint(coh_re, coh_im)
    right_re, right_im = mat_product(far_re, far_im, cadj_re, cadj_im)
    seen_block = observed.reshape(frequency_number, 2, 2, 2, entries_in_tile)
    diff_re = jnp.transpose(seen_block[:, :, :, 0], (1, 2, 3, 0)) - jnp.sum(model_re, axis=-1)
    diff_im = jnp.transpose(seen_block[:, :, :, 1], (1, 2, 3, 0)) - jnp.sum(model_im, axis=-1)
    radj_re, radj_im = adjoint(diff_re, diff_im)
    gnear_re, gnear_im = mat_product(diff_re[..., None], diff_im[..., None], right_re, right_im)
    gfar_re, gfar_im = mat_product(radj_re[..., None], radj_im[..., None], left_re, left_im)
    stacked = jnp.stack((diff_re, diff_im), axis=2)
    resid_block = jnp.transpose(stacked, (4, 0, 1, 2, 3)).reshape(
        frequency_number, 8, entries_in_tile
    )
    return (resid_block, from_matrix(-gnear_re, -gnear_im), from_matrix(-gfar_re, -gfar_im))


def segment_rows(values, stations, row_count):
    inside = (stations >= 0) & (stations < row_count)
    target = jnp.where(inside, stations, row_count)
    return jax.ops.segment_sum(values, target, num_segments=row_count + 1)[:row_count]


def general_shards(pair_uvw_coordinates, directions, brightness, observed, coefficients, station_pair):
    frequency_number = brightness.shape[1]
    dir_count = brightness.shape[2]
    degree_count = coefficients.shape[1] // 8
    stations_dev = coefficients.shape[0]
    pairs_held_here = pair_uvw_coordinates.shape[1]
    powers, freq_ratio = powers_of(frequency_number, degree_count)
    jones_all = evaluate(lax.all_gather(coefficients, "stn", axis=0, tiled=True), powers)
    entries_in_tile = math.gcd(pairs_held_here, 32)
    rotation_number = pairs_held_here // entries_in_tile
    coords_blocks = jnp.transpose(
        pair_uvw_coordinates.reshape(3, rotation_number, entries_in_tile), (1, 0, 2)
    )
    seen_blocks = jnp.transpose(
        observed.reshape(frequency_number, 8, rotation_number, entries_in_tile), (2, 0, 1, 3)
    )
    near_blocks = station_pair[0].reshape(rotation_number, entries_in_tile)
    far_blocks = station_pair[1].reshape(rotation_number, entries_in_tile)

    def visit_block(pieces):
        coords, seen_block, pick_near, pick_far = pieces
        resid_block, slope_first_antenna, slope_second_antenna = baseline_terms(
            jnp.take(jones_all, pick_near, axis=0),
            jnp.take(jones_all, pick_far, axis=0),
            coords,
            directions,
            brightness,
            seen_block,
            freq_ratio,
        )
        slope_first_antenna = contract(slope_first_antenna, powers)
        slope_second_antenna = contract(slope_second_antenna, powers)
        return (
            resid_block,
            slope_first_antenna.reshape(entries_in_tile, -1),
            slope_second_antenna.reshape(entries_in_tile, -1),
        )

    residual_blocks, slope_first_antenna, slope_second_antenna = lax.map(
        visit_block, (coords_blocks, seen_blocks, near_blocks, far_blocks)
    )
    slope_first_antenna = slope_first_antenna.reshape(pairs_held_here, slope_first_antenna.shape[2])
    slope_second_antenna = slope_second_antenna.reshape(
        pairs_held_here, slope_second_antenna.shape[2]
    )
    summed = lax.psum_scatter(
        segment_rows(slope_first_antenna, station_pair[0], lax.axis_size("stn") * stations_dev)
        + segment_rows(slope_second_antenna, station_pair[1], lax.axis_size("stn") * stations_dev),
        "stn",
        scatter_dimension=0,
        tiled=True,
    )
    gradient = summed.reshape(stations_dev, degree_count * 8, dir_count)
    residual = jnp.transpose(residual_blocks, (1, 2, 0, 3)).reshape(
        frequency_number, 8, pairs_held_here
    )
    return (gradient, residual)


def place(n):
    cores = 2 if n % 2 == 0 else 1
    columns = 2 if n % (2 * cores) == 0 else 1
    depth = n // (cores * columns)
    me = lax.axis_index("stn")
    z, rest = lax.div(me, cores * columns), lax.rem(me, cores * columns)
    return depth, columns, cores, z, lax.div(rest, cores), lax.rem(rest, cores)


class Hops:
    def __init__(self, n, send_sem, recv_sem):
        self.depth, self.columns, self.cores, self.z, self.x, self.c = place(n)
        self.send_sem, self.recv_sem = send_sem, recv_sem
        self.copies = {}

    def index(self, dz, dx, dc):
        z = lax.rem(self.z + dz + self.depth, self.depth)
        x = 1 - self.x if dx else self.x
        c = 1 - self.c if dc else self.c
        return (z * self.columns + x) * self.cores + c

    def greet(self):
        barrier = pltpu.get_barrier_semaphore()
        peers = [(d, 0, 0) for d in range(1, self.depth)]
        peers += [(0, 1, 0)] * (self.columns > 1) + [(0, 0, 1)] * (self.cores > 1)
        for peer in peers:
            pl.semaphore_signal(
                barrier, inc=1, device_id={"stn": self.index(*peer)}, device_id_type=MESH
            )
        pl.semaphore_wait(barrier, len(peers))

    def send(self, key, peer, src, dst):
        number = len(self.copies)
        copy = pltpu.make_async_remote_copy(
            src_ref=src,
            dst_ref=dst,
            send_sem=self.send_sem.at[number],
            recv_sem=self.recv_sem.at[number],
            device_id={"stn": self.index(*peer)},
            device_id_type=MESH,
        )
        copy.start()
        self.copies[key] = copy

    def arrived(self, key):
        self.copies[key].wait_recv()

    def settle(self):
        for copy in self.copies.values():
            copy.wait_send()


def gather_kernel(n, own_ref, all_ref, held, send_sem, recv_sem, out_sem):
    hops = Hops(n, send_sem, recv_sem)
    outs = []

    def keep(src, slot):
        out = pltpu.make_async_copy(src, all_ref.at[slot], out_sem.at[len(outs)])
        out.start()
        outs.append(out)

    me = hops.index(0, 0, 0)
    mine = held.at[me]
    hops.greet()
    for d in range(1, hops.depth):
        hops.send(("z", d), (d, 0, 0), own_ref, mine)
    hops.send(("x", 0), (0, 1, 0), own_ref, mine)
    hops.send(("c", 0, 0), (0, 0, 1), own_ref, mine)
    keep(own_ref, me)
    for d in range(1, hops.depth):
        hops.arrived(("z", d))
        slot = hops.index(-d, 0, 0)
        hops.send(("x", d), (0, 1, 0), held.at[slot], held.at[slot])
        hops.send(("c", d, 0), (0, 0, 1), held.at[slot], held.at[slot])
        keep(held.at[slot], slot)
    for d in range(hops.depth):
        hops.arrived(("x", d))
        slot = hops.index(-d, 1, 0)
        hops.send(("c", d, 1), (0, 0, 1), held.at[slot], held.at[slot])
        keep(held.at[slot], slot)
    for dx in range(2):
        for d in range(hops.depth):
            hops.arrived(("c", d, dx))
            slot = hops.index(-d, dx, 1)
            keep(held.at[slot], slot)
    for out in outs:
        out.wait()
    hops.settle()


def scatter_sum_kernel(n, part_ref, sum_ref, own, from_c, from_x, from_z, send_sem, recv_sem, in_sem):
    hops = Hops(n, send_sem, recv_sem)
    order = [(d, dx) for dx in (1, 0) for d in [*range(1, hops.depth), 0]]
    ins = {}
    for k, (d, dx) in enumerate(order):
        ins[d, dx] = pltpu.make_async_copy(
            part_ref.at[hops.index(d, dx, 0)], own.at[dx, d], in_sem.at[k]
        )
        ins[d, dx].start()
    hops.greet()
    for d, dx in order:
        hops.send(
            ("c", d, dx), (0, 0, 1), part_ref.at[hops.index(d, dx, 1)], from_c.at[dx, d]
        )
    for d, dx in order:
        ins[d, dx].wait()
        hops.arrived(("c", d, dx))
        if dx:
            own[dx, d] = own[dx, d] + from_c[dx, d]
            hops.send(("x", d), (0, 1, 0), own.at[dx, d], from_x.at[d])
            continue
        hops.arrived(("x", d))
        total = own[dx, d] + from_c[dx, d] + from_x[d]
        if d:
            own[dx, d] = total
            hops.send(("z", d), (d, 0, 0), own.at[dx, d], from_z.at[d])
    for d in range(1, hops.depth):
        hops.arrived(("z", d))
        total = total + from_z[d]
    sum_ref[...] = total
    hops.settle()


def turn_sin_cos(turns):
    x = math.pi * (turns - jnp.round(turns))
    y = x * x
    s = jnp.full_like(y, -1.0 / math.factorial(11))
    for k in (9, 7, 5, 3, 1):
        s = s * y + (1.0 if k % 4 == 1 else -1.0) / math.factorial(k)
    s = s * x
    c = jnp.full_like(y, 1.0 / math.factorial(12))
    for k in (10, 8, 6, 4, 2, 0):
        c = c * y + (1.0 if k % 4 == 0 else -1.0) / math.factorial(k)
    return 2.0 * (s * c), 1.0 - 2.0 * (s * s)


def scaled(er, ei, m):
    return [(er * r - ei * i, er * i + ei * r) for r, i in m]


def scaled_conj(er, ei, m):
    return [(er * r + ei * i, er * i - ei * r) for r, i in m]


def real_times(left, right):
    return [
        left[2 * i] * right[j] + left[2 * i + 1] * right[2 + j] for i in range(2) for j in range(2)
    ]


def flipped(m):
    return [m[0], m[2], m[1], m[3]]


def both(m):
    return [r + i for r, i in m]


def plus(a, b):
    return [x + y for x, y in zip(a, b)]


def minus(a, b):
    return [x - y for x, y in zip(a, b)]


def local_kernel(
    degree_count,
    together,
    uvw_ref,
    pair_hbm,
    dir_ref,
    bright_ref,
    seen_ref,
    coeff_hbm,
    part_hbm,
    resid_ref,
    pair_ref,
    coeff_ref,
    part_ref,
    jones,
    with_b,
    with_badj,
    grads,
    seen,
    diffs,
    forms,
    turns,
    steps,
    pair_sem,
    table_sem,
):
    channels = bright_ref.shape[1]
    stations = coeff_ref.shape[0]
    chunk = stations // table_sem.shape[0]

    def span_of(s):
        return pl.ds(pl.multiple_of(lax.div(s, chunk) * chunk, chunk), chunk)

    def table_in(s):
        return pltpu.make_async_copy(
            coeff_hbm.at[span_of(s)], coeff_ref.at[span_of(s)], table_sem.at[lax.div(s, chunk)]
        )

    def part_out(s):
        return pltpu.make_async_copy(
            part_ref.at[span_of(s)], part_hbm.at[span_of(s)], table_sem.at[lax.div(s, chunk)]
        )

    for k in range(table_sem.shape[0]):
        table_in(k * chunk).start()
    pair_in = pltpu.make_async_copy(pair_hbm, pair_ref, pair_sem)
    pair_in.start()
    pairs = uvw_ref.shape[1]
    groups = channels // ROWS
    tile = (ROWS, LANES)
    f32 = jnp.float32
    row = lax.broadcasted_iota(jnp.int32, tile, 0)
    lane = lax.broadcasted_iota(jnp.int32, tile, 1)
    span = max(channels - 1, 1)
    xs = [(2.0 * (row + ROWS * g).astype(f32) - (channels - 1)) / span for g in range(groups)]
    ratio = 1.0 + 0.25 * xs[0]
    stride = 0.25 * 2.0 * ROWS / span

    def block(ref, g, lead=()):
        return [
            tuple(
                ref[(*lead, 2 * e + t, pl.ds(ROWS * g, ROWS), slice(None))] for t in range(2)
            )
            for e in range(4)
        ]

    for g in range(groups):
        for comp in range(8):
            seen[comp, pl.ds(ROWS * g, ROWS), :] = seen_ref[
                pl.ds(8 * ROWS * g + comp, ROWS, stride=8), :
            ]
        for e, (re, im) in enumerate(block(bright_ref, g)):
            forms[e, pl.ds(ROWS * g, ROWS), :] = re + im
            forms[4 + e, pl.ds(ROWS * g, ROWS), :] = re - im

    def prepare(s, carry):
        @pl.when(lax.rem(s, chunk) == 0)
        def _():
            table_in(s).wait()

        table = [
            jnp.broadcast_to(coeff_ref[s, pl.ds(i, 1), :], tile) for i in range(8 * degree_count)
        ]
        for g in range(groups):
            rows = pl.ds(ROWS * g, ROWS)
            flat = []
            for comp in range(8):
                value = table[8 * (degree_count - 1) + comp]
                for n in range(degree_count - 2, -1, -1):
                    value = value * xs[g] + table[8 * n + comp]
                flat.append(value)
            jr, ji = flat[0::2], flat[1::2]
            js = plus(jr, ji)
            br, bi = [bright_ref[2 * e, rows, :] for e in range(4)], [
                bright_ref[2 * e + 1, rows, :] for e in range(4)
            ]
            bs, bd = [forms[e, rows, :] for e in range(4)], [
                forms[4 + e, rows, :] for e in range(4)
            ]
            common = real_times(js, br)
            a = (minus(common, real_times(ji, bs)), minus(common, real_times(jr, bd)))
            common = real_times(js, flipped(br))
            d = (
                minus(common, real_times(ji, flipped(bd))),
                minus(common, real_times(jr, flipped(bs))),
            )
            jd = minus(jr, ji)
            for e in range(4):
                for t in range(2):
                    with_b[s, 2 * e + t, rows, :] = a[t][e]
                    with_badj[s, 2 * e + t, rows, :] = d[t][e]
                for t, form in enumerate((jr, js, jd)):
                    jones[s, 4 * t + e, rows, :] = form[e]
                    grads[s, 4 * t + e, rows, :] = jnp.zeros(tile, f32)
        return carry

    lax.fori_loop(0, stations, prepare, 0)
    pair_in.wait()

    l = jnp.broadcast_to(dir_ref[0:1, :], tile)
    m = jnp.broadcast_to(dir_ref[1:2, :], tile)
    depth = jnp.sqrt(1.0 - l * l - m * m) - 1.0

    def measure(b, carry):
        inner = uvw_ref[0, b] * l + uvw_ref[1, b] * m + uvw_ref[2, b] * depth
        turns[pl.ds(b, 1), :] = inner[0:1, :]
        return carry

    lax.fori_loop(0, pairs, measure, 0, unroll=8)

    def step_of(i, carry):
        some = pl.ds(pl.multiple_of(i * ROWS, ROWS), ROWS)
        s, c = turn_sin_cos(stride * turns[some, :])
        steps[0, some, :] = s
        steps[1, some, :] = c
        return carry

    lax.fori_loop(0, pairs // ROWS, step_of, 0)

    def predict(b):
        p, q = pair_ref[0, b], pair_ref[1, b]
        s, c = turn_sin_cos(ratio * jnp.broadcast_to(turns[pl.ds(b, 1), :], tile))
        step_s = jnp.broadcast_to(steps[0, pl.ds(b, 1), :], tile)
        step_c = jnp.broadcast_to(steps[1, pl.ds(b, 1), :], tile)
        er, ei = c, -s
        here = lane == b
        out = []
        for g in range(groups):
            rows = pl.ds(ROWS * g, ROWS)
            if g:
                er, ei = er * step_c + ei * step_s, ei * step_c - er * step_s
            t = scaled(er, ei, block(with_b, g, (p,)))
            tr, ti = [v[0] for v in t], [v[1] for v in t]
            ts = plus(tr, ti)
            jr, js, jd = [
                flipped([jones[q, 4 * k + e, rows, :] for e in range(4)]) for k in range(3)
            ]
            common = real_times(ts, jr)
            model = (minus(common, real_times(ti, jd)), minus(common, real_times(tr, js)))
            diff = ([], [])
            for e in range(4):
                for k in range(2):
                    comp = 2 * e + k
                    term = model[k][e] - jnp.where(here, seen[comp, rows, :], 0.0)
                    total = jnp.broadcast_to(jnp.sum(term, axis=1, keepdims=True), tile)
                    pltpu.store(diffs.at[comp, rows, :], total, mask=here)
                    diff[k].append(total)
            out.append((er, ei, tr, ti, ts, diff))
        return p, q, out

    def deposit(state):
        p, q, out = state
        for g in range(groups):
            rows = pl.ds(ROWS * g, ROWS)
            er, ei, tr, ti, ts, (rr, ri) = out[g]
            u = scaled_conj(er, ei, block(with_badj, g, (q,)))
            ur, ui = [v[0] for v in u], [v[1] for v in u]
            rp, rm = plus(rr, ri), minus(ri, rr)
            near = (real_times(rr, both(u)), real_times(rp, ui), real_times(rm, ur))
            for k in range(3):
                for e in range(4):
                    grads[p, 4 * k + e, rows, :] += near[k][e]
            far = (
                real_times(flipped(rr), ts),
                real_times(flipped(rm), ti),
                real_times(flipped(rp), tr),
            )
            for e in range(4):
                grads[q, e, rows, :] += far[0][e]
                grads[q, 4 + e, rows, :] -= far[1][e]
                grads[q, 8 + e, rows, :] -= far[2][e]

    def visit(i, carry):
        last = predict(i * together)
        for u in range(1, together):
            state = predict(i * together + u)
            deposit(last)
            last = state
        deposit(last)
        return carry

    lax.fori_loop(0, pairs // together, visit, 0)

    def finish(s, carry):
        for comp in range(8):
            terms = []
            for g in range(groups):
                rows = pl.ds(ROWS * g, ROWS)
                first = grads[s, comp // 2, rows, :]
                if comp % 2:
                    terms.append(first + grads[s, 8 + comp // 2, rows, :])
                else:
                    terms.append(first - grads[s, 4 + comp // 2, rows, :])
            for n in range(degree_count):
                if n:
                    terms = [v * x for v, x in zip(terms, xs)]
                part_ref[s, pl.ds(8 * n + comp, 1), :] = jnp.sum(
                    sum(terms[1:], terms[0]), axis=0, keepdims=True
                )

        @pl.when(lax.rem(s, chunk) == chunk - 1)
        def _():
            part_out(s).start()

        return carry

    lax.fori_loop(0, stations, finish, 0)

    for g in range(groups):
        for comp in range(8):
            resid_ref[pl.ds(8 * ROWS * g + comp, ROWS, stride=8), :] = -diffs[
                comp, pl.ds(ROWS * g, ROWS), :
            ]
    for k in range(table_sem.shape[0]):
        part_out(k * chunk).wait()


def gather(own, n):
    return pl.pallas_call(
        functools.partial(gather_kernel, n),
        out_shape=jax.ShapeDtypeStruct((n, *own.shape), own.dtype),
        in_specs=[pl.BlockSpec(memory_space=pltpu.VMEM)],
        out_specs=pl.BlockSpec(memory_space=pltpu.HBM),
        scratch_shapes=[
            pltpu.VMEM((n, *own.shape), own.dtype),
            pltpu.SemaphoreType.DMA((n,)),
            pltpu.SemaphoreType.DMA((n,)),
            pltpu.SemaphoreType.DMA((n,)),
        ],
        compiler_params=pltpu.CompilerParams(collective_id=1, has_side_effects=True),
        name="gather_coefficients",
    )(own)


def scatter_sum(parts, n):
    piece = parts.shape[1:]
    return pl.pallas_call(
        functools.partial(scatter_sum_kernel, n),
        out_shape=jax.ShapeDtypeStruct(piece, parts.dtype),
        in_specs=[pl.BlockSpec(memory_space=pltpu.HBM)],
        out_specs=pl.BlockSpec(memory_space=pltpu.VMEM),
        scratch_shapes=[
            pltpu.VMEM((2, n // 4, *piece), parts.dtype),
            pltpu.VMEM((2, n // 4, *piece), parts.dtype),
            pltpu.VMEM((n // 4, *piece), parts.dtype),
            pltpu.VMEM((n // 4, *piece), parts.dtype),
            pltpu.SemaphoreType.DMA((n,)),
            pltpu.SemaphoreType.DMA((n,)),
            pltpu.SemaphoreType.DMA((n,)),
        ],
        compiler_params=pltpu.CompilerParams(collective_id=2, has_side_effects=True),
        name="sum_gradient",
    )(parts)


def compact_shards(uvw, directions, brightness, observed, coefficients, pair):
    n = lax.axis_size("stn")
    channels, dirs = brightness.shape[1:]
    held, rows = coefficients.shape[:2]
    pairs = uvw.shape[1]
    table = gather(coefficients, n).reshape(n * held, rows, dirs)
    vmem = pl.BlockSpec(memory_space=pltpu.VMEM)
    away = pl.BlockSpec(memory_space=pltpu.HBM)
    smem = pl.BlockSpec(memory_space=pltpu.SMEM)

    def per_station(forms):
        return pltpu.VMEM((n * held, forms, channels, dirs), jnp.float32)

    per_pair = pltpu.VMEM((8, channels, pairs), jnp.float32)
    partial, residual = pl.pallas_call(
        functools.partial(local_kernel, rows // 8, 4),
        out_shape=(
            jax.ShapeDtypeStruct(table.shape, jnp.float32),
            jax.ShapeDtypeStruct((channels * 8, pairs), jnp.float32),
        ),
        in_specs=[smem, away, vmem, vmem, vmem, away],
        out_specs=(away, vmem),
        scratch_shapes=[pltpu.SMEM(pair.shape, pair.dtype)]
        + [pltpu.VMEM(table.shape, jnp.float32)] * 2
        + [per_station(12), per_station(8), per_station(8), per_station(12)]
        + [per_pair] * 2
        + [
            pltpu.VMEM((8, channels, dirs), jnp.float32),
            pltpu.VMEM((pairs, dirs), jnp.float32),
            pltpu.VMEM((2, pairs, dirs), jnp.float32),
        ]
        + [pltpu.SemaphoreType.DMA, pltpu.SemaphoreType.DMA((4,))],
        compiler_params=pltpu.CompilerParams(vmem_limit_bytes=VMEM_BUDGET),
        name="predict_and_slope",
    )(uvw, pair, directions, brightness, observed.reshape(channels * 8, pairs), table)
    gradient = scatter_sum(partial.reshape(n, held, rows, dirs), n)
    return gradient, residual.reshape(channels, 8, pairs)


def shards(uvw, directions, brightness, observed, coefficients, pair):
    channels, dirs = brightness.shape[1:]
    stations = lax.axis_size("stn") * coefficients.shape[0]
    fits = lax.axis_size("stn") % 4 == 0 and 40 * stations * channels * dirs * 4 <= VMEM_BUDGET // 2
    if fits and dirs == LANES and uvw.shape[1] == LANES and channels % ROWS == 0:
        return compact_shards(uvw, directions, brightness, observed, coefficients, pair)
    return general_shards(uvw, directions, brightness, observed, coefficients, pair)


def solution(mesh):
    placed = (
        P(None, ("grp", "stn")),
        P(),
        P(),
        P(None, None, ("grp", "stn")),
        P(("grp", "stn"), None, None),
        P(None, ("grp", "stn")),
    )
    return jax.shard_map(
        shards,
        mesh=mesh,
        in_specs=placed,
        out_specs=(P(("grp", "stn"), None, None), P(None, None, ("grp", "stn"))),
        check_vma=False,
    )
```

```python
import functools
import math

import jax
import jax.numpy as jnp
from jax import lax
from jax.experimental import pallas as pl
from jax.experimental.pallas import tpu as pltpu
from jax.sharding import PartitionSpec as P

MESH = pl.DeviceIdType.MESH
LANES = 128
ROWS = 8
VMEM_BUDGET = 64512 * 1024


def powers_of(frequency_number, degree_count):
    channel_pos = jnp.arange(frequency_number, dtype=jnp.float32)
    centre = (2.0 * channel_pos - (frequency_number - 1)) / max(frequency_number - 1, 1)
    levels = [jnp.ones_like(centre)]
    for degree in range(1, degree_count):
        levels.append(levels[-1] * centre)
    return (jnp.stack(levels), 1.0 + 0.25 * centre)


def evaluate(coeff_table, powers):
    degree_count = powers.shape[0]
    shaped = coeff_table.reshape(coeff_table.shape[0], degree_count, 8, coeff_table.shape[2])
    result = shaped[:, 0][:, None] * powers[0][None, :, None, None]
    for degree in range(1, degree_count):
        result = result + shaped[:, degree][:, None] * powers[degree][None, :, None, None]
    return result


def contract(grads, powers):
    pieces = [
        jnp.sum(grads * powers[degree][None, :, None, None], axis=1)
        for degree in range(powers.shape[0])
    ]
    stacked = jnp.stack(pieces, axis=1)
    return stacked.reshape(stacked.shape[0], stacked.shape[1] * 8, stacked.shape[3])


def mat_product(left_re, left_im, right_re, right_im):
    first_re = left_re[:, 0:1] * right_re[0:1] - left_im[:, 0:1] * right_im[0:1]
    second_re = left_re[:, 1:2] * right_re[1:2] - left_im[:, 1:2] * right_im[1:2]
    first_im = left_re[:, 0:1] * right_im[0:1] + left_im[:, 0:1] * right_re[0:1]
    second_im = left_re[:, 1:2] * right_im[1:2] + left_im[:, 1:2] * right_re[1:2]
    return (first_re + second_re, first_im + second_im)


def adjoint(matrix_re, matrix_im):
    return (jnp.swapaxes(matrix_re, 0, 1), -jnp.swapaxes(matrix_im, 0, 1))


def to_matrix(jones_rows):
    shaped = jones_rows.reshape(
        jones_rows.shape[0], jones_rows.shape[1], 2, 2, 2, jones_rows.shape[3]
    )
    real_part = jnp.transpose(shaped[:, :, :, :, 0], (2, 3, 0, 1, 4))
    imag_part = jnp.transpose(shaped[:, :, :, :, 1], (2, 3, 0, 1, 4))
    return (real_part, imag_part)


def from_matrix(real_part, imag_part):
    stacked = jnp.stack((real_part, imag_part), axis=2)
    reordered = jnp.transpose(stacked, (3, 4, 0, 1, 2, 5))
    return reordered.reshape(reordered.shape[0], reordered.shape[1], 8, reordered.shape[5])


def baseline_terms(jones_near, jones_far, coords, directions, brightness, observed, freq_ratio):
    frequency_number = brightness.shape[1]
    dir_count = brightness.shape[2]
    entries_in_tile = coords.shape[1]
    depth_term = jnp.sqrt(1.0 - directions[0] * directions[0] - directions[1] * directions[1]) - 1.0
    inner_sum = (
        coords[0][:, None] * directions[0][None, :]
        + coords[1][:, None] * directions[1][None, :]
        + coords[2][:, None] * depth_term[None, :]
    )
    phase_angle = 2.0 * math.pi * freq_ratio[None, :, None] * inner_sum[:, None, :]
    cosine = jnp.cos(phase_angle)
    sine_part = jnp.sin(phase_angle)
    bright = brightness.reshape(2, 2, 2, frequency_number, dir_count)
    bright_re = bright[:, :, 0][:, :, None]
    bright_im = bright[:, :, 1][:, :, None]
    coh_re = bright_re * cosine + bright_im * sine_part
    coh_im = bright_im * cosine - bright_re * sine_part
    near_re, near_im = to_matrix(jones_near)
    far_re, far_im = to_matrix(jones_far)
    left_re, left_im = mat_product(near_re, near_im, coh_re, coh_im)
    fadj_re, fadj_im = adjoint(far_re, far_im)
    model_re, model_im = mat_product(left_re, left_im, fadj_re, fadj_im)
    cadj_re, cadj_im = adjoint(coh_re, coh_im)
    right_re, right_im = mat_product(far_re, far_im, cadj_re, cadj_im)
    seen_block = observed.reshape(frequency_number, 2, 2, 2, entries_in_tile)
    diff_re = jnp.transpose(seen_block[:, :, :, 0], (1, 2, 3, 0)) - jnp.sum(model_re, axis=-1)
    diff_im = jnp.transpose(seen_block[:, :, :, 1], (1, 2, 3, 0)) - jnp.sum(model_im, axis=-1)
    radj_re, radj_im = adjoint(diff_re, diff_im)
    gnear_re, gnear_im = mat_product(diff_re[..., None], diff_im[..., None], right_re, right_im)
    gfar_re, gfar_im = mat_product(radj_re[..., None], radj_im[..., None], left_re, left_im)
    stacked = jnp.stack((diff_re, diff_im), axis=2)
    resid_block = jnp.transpose(stacked, (4, 0, 1, 2, 3)).reshape(
        frequency_number, 8, entries_in_tile
    )
    return (resid_block, from_matrix(-gnear_re, -gnear_im), from_matrix(-gfar_re, -gfar_im))


def segment_rows(values, stations, row_count):
    inside = (stations >= 0) & (stations < row_count)
    target = jnp.where(inside, stations, row_count)
    return jax.ops.segment_sum(values, target, num_segments=row_count + 1)[:row_count]


def general_shards(pair_uvw_coordinates, directions, brightness, observed, coefficients, station_pair):
    frequency_number = brightness.shape[1]
    dir_count = brightness.shape[2]
    degree_count = coefficients.shape[1] // 8
    stations_dev = coefficients.shape[0]
    pairs_held_here = pair_uvw_coordinates.shape[1]
    powers, freq_ratio = powers_of(frequency_number, degree_count)
    jones_all = evaluate(lax.all_gather(coefficients, "stn", axis=0, tiled=True), powers)
    entries_in_tile = math.gcd(pairs_held_here, 32)
    rotation_number = pairs_held_here // entries_in_tile
    coords_blocks = jnp.transpose(
        pair_uvw_coordinates.reshape(3, rotation_number, entries_in_tile), (1, 0, 2)
    )
    seen_blocks = jnp.transpose(
        observed.reshape(frequency_number, 8, rotation_number, entries_in_tile), (2, 0, 1, 3)
    )
    near_blocks = station_pair[0].reshape(rotation_number, entries_in_tile)
    far_blocks = station_pair[1].reshape(rotation_number, entries_in_tile)

    def visit_block(pieces):
        coords, seen_block, pick_near, pick_far = pieces
        resid_block, slope_first_antenna, slope_second_antenna = baseline_terms(
            jnp.take(jones_all, pick_near, axis=0),
            jnp.take(jones_all, pick_far, axis=0),
            coords,
            directions,
            brightness,
            seen_block,
            freq_ratio,
        )
        slope_first_antenna = contract(slope_first_antenna, powers)
        slope_second_antenna = contract(slope_second_antenna, powers)
        return (
            resid_block,
            slope_first_antenna.reshape(entries_in_tile, -1),
            slope_second_antenna.reshape(entries_in_tile, -1),
        )

    residual_blocks, slope_first_antenna, slope_second_antenna = lax.map(
        visit_block, (coords_blocks, seen_blocks, near_blocks, far_blocks)
    )
    slope_first_antenna = slope_first_antenna.reshape(pairs_held_here, slope_first_antenna.shape[2])
    slope_second_antenna = slope_second_antenna.reshape(
        pairs_held_here, slope_second_antenna.shape[2]
    )
    summed = lax.psum_scatter(
        segment_rows(slope_first_antenna, station_pair[0], lax.axis_size("stn") * stations_dev)
        + segment_rows(slope_second_antenna, station_pair[1], lax.axis_size("stn") * stations_dev),
        "stn",
        scatter_dimension=0,
        tiled=True,
    )
    gradient = summed.reshape(stations_dev, degree_count * 8, dir_count)
    residual = jnp.transpose(residual_blocks, (1, 2, 0, 3)).reshape(
        frequency_number, 8, pairs_held_here
    )
    return (gradient, residual)


def place(n):
    cores = 2 if n % 2 == 0 else 1
    columns = 2 if n % (2 * cores) == 0 else 1
    depth = n // (cores * columns)
    me = lax.axis_index("stn")
    z, rest = lax.div(me, cores * columns), lax.rem(me, cores * columns)
    return depth, columns, cores, z, lax.div(rest, cores), lax.rem(rest, cores)


class Hops:
    def __init__(self, n, send_sem, recv_sem):
        self.depth, self.columns, self.cores, self.z, self.x, self.c = place(n)
        self.send_sem, self.recv_sem = send_sem, recv_sem
        self.copies = {}

    def index(self, dz, dx, dc):
        z = lax.rem(self.z + dz + self.depth, self.depth)
        x = 1 - self.x if dx else self.x
        c = 1 - self.c if dc else self.c
        return (z * self.columns + x) * self.cores + c

    def greet(self):
        barrier = pltpu.get_barrier_semaphore()
        peers = [(d, 0, 0) for d in range(1, self.depth)]
        peers += [(0, 1, 0)] * (self.columns > 1) + [(0, 0, 1)] * (self.cores > 1)
        for peer in peers:
            pl.semaphore_signal(
                barrier, inc=1, device_id={"stn": self.index(*peer)}, device_id_type=MESH
            )
        pl.semaphore_wait(barrier, len(peers))

    def send(self, key, peer, src, dst):
        number = len(self.copies)
        copy = pltpu.make_async_remote_copy(
            src_ref=src,
            dst_ref=dst,
            send_sem=self.send_sem.at[number],
            recv_sem=self.recv_sem.at[number],
            device_id={"stn": self.index(*peer)},
            device_id_type=MESH,
        )
        copy.start()
        self.copies[key] = copy

    def arrived(self, key):
        self.copies[key].wait_recv()

    def settle(self):
        for copy in self.copies.values():
            copy.wait_send()


def gather_kernel(n, own_ref, all_ref, held, send_sem, recv_sem, out_sem):
    hops = Hops(n, send_sem, recv_sem)
    outs = []

    def keep(src, slot):
        out = pltpu.make_async_copy(src, all_ref.at[slot], out_sem.at[len(outs)])
        out.start()
        outs.append(out)

    me = hops.index(0, 0, 0)
    mine = held.at[me]
    hops.greet()
    for d in range(1, hops.depth):
        hops.send(("z", d), (d, 0, 0), own_ref, mine)
    hops.send(("x", 0), (0, 1, 0), own_ref, mine)
    hops.send(("c", 0, 0), (0, 0, 1), own_ref, mine)
    keep(own_ref, me)
    for d in range(1, hops.depth):
        hops.arrived(("z", d))
        slot = hops.index(-d, 0, 0)
        hops.send(("x", d), (0, 1, 0), held.at[slot], held.at[slot])
        hops.send(("c", d, 0), (0, 0, 1), held.at[slot], held.at[slot])
        keep(held.at[slot], slot)
    for d in range(hops.depth):
        hops.arrived(("x", d))
        slot = hops.index(-d, 1, 0)
        hops.send(("c", d, 1), (0, 0, 1), held.at[slot], held.at[slot])
        keep(held.at[slot], slot)
    for dx in range(2):
        for d in range(hops.depth):
            hops.arrived(("c", d, dx))
            slot = hops.index(-d, dx, 1)
            keep(held.at[slot], slot)
    for out in outs:
        out.wait()
    hops.settle()


def scatter_sum_kernel(n, part_ref, sum_ref, own, from_c, from_x, from_z, send_sem, recv_sem, in_sem):
    hops = Hops(n, send_sem, recv_sem)
    order = [(d, dx) for dx in (1, 0) for d in [*range(1, hops.depth), 0]]
    ins = {}
    for k, (d, dx) in enumerate(order):
        ins[d, dx] = pltpu.make_async_copy(
            part_ref.at[hops.index(d, dx, 0)], own.at[dx, d], in_sem.at[k]
        )
        ins[d, dx].start()
    hops.greet()
    for d, dx in order:
        hops.send(
            ("c", d, dx), (0, 0, 1), part_ref.at[hops.index(d, dx, 1)], from_c.at[dx, d]
        )
    for d, dx in order:
        ins[d, dx].wait()
        hops.arrived(("c", d, dx))
        if dx:
            own[dx, d] = own[dx, d] + from_c[dx, d]
            hops.send(("x", d), (0, 1, 0), own.at[dx, d], from_x.at[d])
            continue
        hops.arrived(("x", d))
        total = own[dx, d] + from_c[dx, d] + from_x[d]
        if d:
            own[dx, d] = total
            hops.send(("z", d), (d, 0, 0), own.at[dx, d], from_z.at[d])
    for d in range(1, hops.depth):
        hops.arrived(("z", d))
        total = total + from_z[d]
    sum_ref[...] = total
    hops.settle()


def turn_sin_cos(turns):
    x = math.pi * (turns - jnp.round(turns))
    y = x * x
    s = jnp.full_like(y, -1.0 / math.factorial(11))
    for k in (9, 7, 5, 3, 1):
        s = s * y + (1.0 if k % 4 == 1 else -1.0) / math.factorial(k)
    s = s * x
    c = jnp.full_like(y, 1.0 / math.factorial(12))
    for k in (10, 8, 6, 4, 2, 0):
        c = c * y + (1.0 if k % 4 == 0 else -1.0) / math.factorial(k)
    return 2.0 * (s * c), 1.0 - 2.0 * (s * s)


def times(left, right):
    out = []
    for i in range(2):
        for j in range(2):
            (ar, ai), (br, bi) = left[2 * i], right[j]
            (cr, ci), (dr, di) = left[2 * i + 1], right[2 + j]
            out.append(
                (
                    (ar * br - ai * bi) + (cr * dr - ci * di),
                    (ar * bi + ai * br) + (cr * di + ci * dr),
                )
            )
    return out


def times_adj(left, right):
    out = []
    for i in range(2):
        for j in range(2):
            (ar, ai), (br, bi) = left[2 * i], right[2 * j]
            (cr, ci), (dr, di) = left[2 * i + 1], right[2 * j + 1]
            out.append(
                (
                    (ar * br + ai * bi) + (cr * dr + ci * di),
                    (ai * br - ar * bi) + (ci * dr - cr * di),
                )
            )
    return out


def adj_times(left, right):
    out = []
    for i in range(2):
        for j in range(2):
            (ar, ai), (br, bi) = left[i], right[j]
            (cr, ci), (dr, di) = left[2 + i], right[2 + j]
            out.append(
                (
                    (ar * br + ai * bi) + (cr * dr + ci * di),
                    (ar * bi - ai * br) + (cr * di - ci * dr),
                )
            )
    return out


def scaled(er, ei, m):
    return [(er * r - ei * i, er * i + ei * r) for r, i in m]


def scaled_conj(er, ei, m):
    return [(er * r + ei * i, er * i - ei * r) for r, i in m]


def local_kernel(
    degree_count,
    together,
    uvw_ref,
    pair_hbm,
    dir_ref,
    bright_ref,
    seen_ref,
    coeff_hbm,
    part_hbm,
    resid_ref,
    pair_ref,
    coeff_ref,
    part_ref,
    jones,
    with_b,
    with_badj,
    grads,
    seen,
    diffs,
    pair_sem,
    table_sem,
):
    channels = bright_ref.shape[1]
    stations = coeff_ref.shape[0]
    chunk = stations // table_sem.shape[0]

    def span_of(s):
        return pl.ds(pl.multiple_of(lax.div(s, chunk) * chunk, chunk), chunk)

    def table_in(s):
        return pltpu.make_async_copy(
            coeff_hbm.at[span_of(s)], coeff_ref.at[span_of(s)], table_sem.at[lax.div(s, chunk)]
        )

    def part_out(s):
        return pltpu.make_async_copy(
            part_ref.at[span_of(s)], part_hbm.at[span_of(s)], table_sem.at[lax.div(s, chunk)]
        )

    for k in range(table_sem.shape[0]):
        table_in(k * chunk).start()
    pair_in = pltpu.make_async_copy(pair_hbm, pair_ref, pair_sem)
    pair_in.start()
    pairs = uvw_ref.shape[1]
    groups = channels // ROWS
    tile = (ROWS, LANES)
    f32 = jnp.float32
    row = lax.broadcasted_iota(jnp.int32, tile, 0)
    lane = lax.broadcasted_iota(jnp.int32, tile, 1)
    span = max(channels - 1, 1)
    xs = [(2.0 * (row + ROWS * g).astype(f32) - (channels - 1)) / span for g in range(groups)]
    ratio = 1.0 + 0.25 * xs[0]
    stride = 0.25 * 2.0 * ROWS / span

    def block(ref, g, lead=()):
        return [
            tuple(
                ref[(*lead, 2 * e + t, pl.ds(ROWS * g, ROWS), slice(None))] for t in range(2)
            )
            for e in range(4)
        ]

    for g in range(groups):
        for comp in range(8):
            seen[comp, pl.ds(ROWS * g, ROWS), :] = seen_ref[
                pl.ds(8 * ROWS * g + comp, ROWS, stride=8), :
            ]

    def prepare(s, carry):
        @pl.when(lax.rem(s, chunk) == 0)
        def _():
            table_in(s).wait()

        table = [
            jnp.broadcast_to(coeff_ref[s, pl.ds(i, 1), :], tile) for i in range(8 * degree_count)
        ]
        for g in range(groups):
            rows = pl.ds(ROWS * g, ROWS)
            flat = []
            for comp in range(8):
                value = table[8 * (degree_count - 1) + comp]
                for n in range(degree_count - 2, -1, -1):
                    value = value * xs[g] + table[8 * n + comp]
                flat.append(value)
            j = [(flat[2 * e], flat[2 * e + 1]) for e in range(4)]
            b = block(bright_ref, g)
            a = times(j, b)
            d = times_adj(j, b)
            for e in range(4):
                for t in range(2):
                    jones[s, 2 * e + t, rows, :] = j[e][t]
                    with_b[s, 2 * e + t, rows, :] = a[e][t]
                    with_badj[s, 2 * e + t, rows, :] = d[e][t]
                    grads[s, 2 * e + t, rows, :] = jnp.zeros(tile, f32)
        return carry

    lax.fori_loop(0, stations, prepare, 0)
    pair_in.wait()

    l = jnp.broadcast_to(dir_ref[0:1, :], tile)
    m = jnp.broadcast_to(dir_ref[1:2, :], tile)
    depth = jnp.sqrt(1.0 - l * l - m * m) - 1.0

    def predict(b):
        p, q = pair_ref[0, b], pair_ref[1, b]
        inner = uvw_ref[0, b] * l + uvw_ref[1, b] * m + uvw_ref[2, b] * depth
        s, c = turn_sin_cos(ratio * inner)
        step_s, step_c = turn_sin_cos(stride * inner)
        er, ei = c, -s
        here = lane == b
        out = []
        for g in range(groups):
            if g:
                er, ei = er * step_c + ei * step_s, ei * step_c - er * step_s
            t = scaled(er, ei, block(with_b, g, (p,)))
            model = times_adj(t, block(jones, g, (q,)))
            rows = pl.ds(ROWS * g, ROWS)
            diff = []
            for e in range(4):
                pieces = []
                for k in range(2):
                    comp = 2 * e + k
                    term = model[e][k] - jnp.where(here, seen[comp, rows, :], 0.0)
                    total = jnp.broadcast_to(jnp.sum(term, axis=1, keepdims=True), tile)
                    pltpu.store(diffs.at[comp, rows, :], total, mask=here)
                    pieces.append(total)
                diff.append(tuple(pieces))
            out.append((er, ei, t, diff))
        return p, q, out

    def deposit(state):
        p, q, out = state
        for g in range(groups):
            rows = pl.ds(ROWS * g, ROWS)
            er, ei, t, diff = out[g]
            near = times(diff, scaled_conj(er, ei, block(with_badj, g, (q,))))
            far = adj_times(diff, t)
            for station, slope in ((p, near), (q, far)):
                for e in range(4):
                    for k in range(2):
                        grads[station, 2 * e + k, rows, :] += slope[e][k]

    def visit(i, carry):
        last = predict(i * together)
        for u in range(1, together):
            state = predict(i * together + u)
            deposit(last)
            last = state
        deposit(last)
        return carry

    lax.fori_loop(0, pairs // together, visit, 0)

    def finish(s, carry):
        for comp in range(8):
            terms = [grads[s, comp, pl.ds(ROWS * g, ROWS), :] for g in range(groups)]
            for n in range(degree_count):
                if n:
                    terms = [v * x for v, x in zip(terms, xs)]
                part_ref[s, pl.ds(8 * n + comp, 1), :] = jnp.sum(
                    sum(terms[1:], terms[0]), axis=0, keepdims=True
                )

        @pl.when(lax.rem(s, chunk) == chunk - 1)
        def _():
            part_out(s).start()

        return carry

    lax.fori_loop(0, stations, finish, 0)

    for g in range(groups):
        for comp in range(8):
            resid_ref[pl.ds(8 * ROWS * g + comp, ROWS, stride=8), :] = -diffs[
                comp, pl.ds(ROWS * g, ROWS), :
            ]
    for k in range(table_sem.shape[0]):
        part_out(k * chunk).wait()


def gather(own, n):
    return pl.pallas_call(
        functools.partial(gather_kernel, n),
        out_shape=jax.ShapeDtypeStruct((n, *own.shape), own.dtype),
        in_specs=[pl.BlockSpec(memory_space=pltpu.VMEM)],
        out_specs=pl.BlockSpec(memory_space=pltpu.HBM),
        scratch_shapes=[
            pltpu.VMEM((n, *own.shape), own.dtype),
            pltpu.SemaphoreType.DMA((n,)),
            pltpu.SemaphoreType.DMA((n,)),
            pltpu.SemaphoreType.DMA((n,)),
        ],
        compiler_params=pltpu.CompilerParams(collective_id=1, has_side_effects=True, vmem_limit_bytes=VMEM_BUDGET),
        name="gather_coefficients",
    )(own)


def scatter_sum(parts, n):
    piece = parts.shape[1:]
    return pl.pallas_call(
        functools.partial(scatter_sum_kernel, n),
        out_shape=jax.ShapeDtypeStruct(piece, parts.dtype),
        in_specs=[pl.BlockSpec(memory_space=pltpu.HBM)],
        out_specs=pl.BlockSpec(memory_space=pltpu.VMEM),
        scratch_shapes=[
            pltpu.VMEM((2, n // 4, *piece), parts.dtype),
            pltpu.VMEM((2, n // 4, *piece), parts.dtype),
            pltpu.VMEM((n // 4, *piece), parts.dtype),
            pltpu.VMEM((n // 4, *piece), parts.dtype),
            pltpu.SemaphoreType.DMA((n,)),
            pltpu.SemaphoreType.DMA((n,)),
            pltpu.SemaphoreType.DMA((n,)),
        ],
        compiler_params=pltpu.CompilerParams(collective_id=2, has_side_effects=True, vmem_limit_bytes=VMEM_BUDGET),
        name="sum_gradient",
    )(parts)


def compact_shards(uvw, directions, brightness, observed, coefficients, pair):
    n = lax.axis_size("stn")
    channels, dirs = brightness.shape[1:]
    held, rows = coefficients.shape[:2]
    pairs = uvw.shape[1]
    table = gather(coefficients, n).reshape(n * held, rows, dirs)
    vmem = pl.BlockSpec(memory_space=pltpu.VMEM)
    away = pl.BlockSpec(memory_space=pltpu.HBM)
    smem = pl.BlockSpec(memory_space=pltpu.SMEM)
    per_station = pltpu.VMEM((n * held, 8, channels, dirs), jnp.float32)
    per_pair = pltpu.VMEM((8, channels, pairs), jnp.float32)
    partial, residual = pl.pallas_call(
        functools.partial(local_kernel, rows // 8, 4),
        out_shape=(
            jax.ShapeDtypeStruct(table.shape, jnp.float32),
            jax.ShapeDtypeStruct((channels * 8, pairs), jnp.float32),
        ),
        in_specs=[smem, away, vmem, vmem, vmem, away],
        out_specs=(away, vmem),
        scratch_shapes=[pltpu.SMEM(pair.shape, pair.dtype)]
        + [pltpu.VMEM(table.shape, jnp.float32)] * 2
        + [per_station] * 4
        + [per_pair] * 2
        + [pltpu.SemaphoreType.DMA, pltpu.SemaphoreType.DMA((4,))],
        compiler_params=pltpu.CompilerParams(vmem_limit_bytes=VMEM_BUDGET),
        name="predict_and_slope",
    )(uvw, pair, directions, brightness, observed.reshape(channels * 8, pairs), table)
    gradient = scatter_sum(partial.reshape(n, held, rows, dirs), n)
    return gradient, residual.reshape(channels, 8, pairs)


def shards(uvw, directions, brightness, observed, coefficients, pair):
    channels, dirs = brightness.shape[1:]
    stations = lax.axis_size("stn") * coefficients.shape[0]
    fits = lax.axis_size("stn") % 4 == 0 and 4 * stations * 8 * channels * dirs * 4 <= 22 * 1024 * 1024
    if fits and dirs == LANES and uvw.shape[1] == LANES and channels % ROWS == 0:
        return compact_shards(uvw, directions, brightness, observed, coefficients, pair)
    return general_shards(uvw, directions, brightness, observed, coefficients, pair)


def solution(mesh):
    placed = (
        P(None, ("grp", "stn")),
        P(),
        P(),
        P(None, None, ("grp", "stn")),
        P(("grp", "stn"), None, None),
        P(None, ("grp", "stn")),
    )
    return jax.shard_map(
        shards,
        mesh=mesh,
        in_specs=placed,
        out_specs=(P(("grp", "stn"), None, None), P(None, None, ("grp", "stn"))),
        check_vma=False,
    )
```

```python
import functools
import math

import jax
import jax.numpy as jnp
from jax import lax
from jax.experimental import pallas as pl
from jax.experimental.pallas import tpu as pltpu
from jax.sharding import PartitionSpec as P

MESH = pl.DeviceIdType.MESH
LANES = 128
ROWS = 8
VMEM_BUDGET = 63 * 1024 * 1024


def powers_of(frequency_number, degree_count):
    channel_pos = jnp.arange(frequency_number, dtype=jnp.float32)
    centre = (2.0 * channel_pos - (frequency_number - 1)) / max(frequency_number - 1, 1)
    levels = [jnp.ones_like(centre)]
    for degree in range(1, degree_count):
        levels.append(levels[-1] * centre)
    return (jnp.stack(levels), 1.0 + 0.25 * centre)


def evaluate(coeff_table, powers):
    degree_count = powers.shape[0]
    shaped = coeff_table.reshape(coeff_table.shape[0], degree_count, 8, coeff_table.shape[2])
    result = shaped[:, 0][:, None] * powers[0][None, :, None, None]
    for degree in range(1, degree_count):
        result = result + shaped[:, degree][:, None] * powers[degree][None, :, None, None]
    return result


def contract(grads, powers):
    pieces = [
        jnp.sum(grads * powers[degree][None, :, None, None], axis=1)
        for degree in range(powers.shape[0])
    ]
    stacked = jnp.stack(pieces, axis=1)
    return stacked.reshape(stacked.shape[0], stacked.shape[1] * 8, stacked.shape[3])


def mat_product(left_re, left_im, right_re, right_im):
    first_re = left_re[:, 0:1] * right_re[0:1] - left_im[:, 0:1] * right_im[0:1]
    second_re = left_re[:, 1:2] * right_re[1:2] - left_im[:, 1:2] * right_im[1:2]
    first_im = left_re[:, 0:1] * right_im[0:1] + left_im[:, 0:1] * right_re[0:1]
    second_im = left_re[:, 1:2] * right_im[1:2] + left_im[:, 1:2] * right_re[1:2]
    return (first_re + second_re, first_im + second_im)


def adjoint(matrix_re, matrix_im):
    return (jnp.swapaxes(matrix_re, 0, 1), -jnp.swapaxes(matrix_im, 0, 1))


def to_matrix(jones_rows):
    shaped = jones_rows.reshape(
        jones_rows.shape[0], jones_rows.shape[1], 2, 2, 2, jones_rows.shape[3]
    )
    real_part = jnp.transpose(shaped[:, :, :, :, 0], (2, 3, 0, 1, 4))
    imag_part = jnp.transpose(shaped[:, :, :, :, 1], (2, 3, 0, 1, 4))
    return (real_part, imag_part)


def from_matrix(real_part, imag_part):
    stacked = jnp.stack((real_part, imag_part), axis=2)
    reordered = jnp.transpose(stacked, (3, 4, 0, 1, 2, 5))
    return reordered.reshape(reordered.shape[0], reordered.shape[1], 8, reordered.shape[5])


def baseline_terms(jones_near, jones_far, coords, directions, brightness, observed, freq_ratio):
    frequency_number = brightness.shape[1]
    dir_count = brightness.shape[2]
    entries_in_tile = coords.shape[1]
    depth_term = jnp.sqrt(1.0 - directions[0] * directions[0] - directions[1] * directions[1]) - 1.0
    inner_sum = (
        coords[0][:, None] * directions[0][None, :]
        + coords[1][:, None] * directions[1][None, :]
        + coords[2][:, None] * depth_term[None, :]
    )
    phase_angle = 2.0 * math.pi * freq_ratio[None, :, None] * inner_sum[:, None, :]
    cosine = jnp.cos(phase_angle)
    sine_part = jnp.sin(phase_angle)
    bright = brightness.reshape(2, 2, 2, frequency_number, dir_count)
    bright_re = bright[:, :, 0][:, :, None]
    bright_im = bright[:, :, 1][:, :, None]
    coh_re = bright_re * cosine + bright_im * sine_part
    coh_im = bright_im * cosine - bright_re * sine_part
    near_re, near_im = to_matrix(jones_near)
    far_re, far_im = to_matrix(jones_far)
    left_re, left_im = mat_product(near_re, near_im, coh_re, coh_im)
    fadj_re, fadj_im = adjoint(far_re, far_im)
    model_re, model_im = mat_product(left_re, left_im, fadj_re, fadj_im)
    cadj_re, cadj_im = adjoint(coh_re, coh_im)
    right_re, right_im = mat_product(far_re, far_im, cadj_re, cadj_im)
    seen_block = observed.reshape(frequency_number, 2, 2, 2, entries_in_tile)
    diff_re = jnp.transpose(seen_block[:, :, :, 0], (1, 2, 3, 0)) - jnp.sum(model_re, axis=-1)
    diff_im = jnp.transpose(seen_block[:, :, :, 1], (1, 2, 3, 0)) - jnp.sum(model_im, axis=-1)
    radj_re, radj_im = adjoint(diff_re, diff_im)
    gnear_re, gnear_im = mat_product(diff_re[..., None], diff_im[..., None], right_re, right_im)
    gfar_re, gfar_im = mat_product(radj_re[..., None], radj_im[..., None], left_re, left_im)
    stacked = jnp.stack((diff_re, diff_im), axis=2)
    resid_block = jnp.transpose(stacked, (4, 0, 1, 2, 3)).reshape(
        frequency_number, 8, entries_in_tile
    )
    return (resid_block, from_matrix(-gnear_re, -gnear_im), from_matrix(-gfar_re, -gfar_im))


def segment_rows(values, stations, row_count):
    inside = (stations >= 0) & (stations < row_count)
    target = jnp.where(inside, stations, row_count)
    return jax.ops.segment_sum(values, target, num_segments=row_count + 1)[:row_count]


def general_shards(pair_uvw_coordinates, directions, brightness, observed, coefficients, station_pair):
    frequency_number = brightness.shape[1]
    dir_count = brightness.shape[2]
    degree_count = coefficients.shape[1] // 8
    stations_dev = coefficients.shape[0]
    pairs_held_here = pair_uvw_coordinates.shape[1]
    powers, freq_ratio = powers_of(frequency_number, degree_count)
    jones_all = evaluate(lax.all_gather(coefficients, "stn", axis=0, tiled=True), powers)
    entries_in_tile = math.gcd(pairs_held_here, 32)
    rotation_number = pairs_held_here // entries_in_tile
    coords_blocks = jnp.transpose(
        pair_uvw_coordinates.reshape(3, rotation_number, entries_in_tile), (1, 0, 2)
    )
    seen_blocks = jnp.transpose(
        observed.reshape(frequency_number, 8, rotation_number, entries_in_tile), (2, 0, 1, 3)
    )
    near_blocks = station_pair[0].reshape(rotation_number, entries_in_tile)
    far_blocks = station_pair[1].reshape(rotation_number, entries_in_tile)

    def visit_block(pieces):
        coords, seen_block, pick_near, pick_far = pieces
        resid_block, slope_first_antenna, slope_second_antenna = baseline_terms(
            jnp.take(jones_all, pick_near, axis=0),
            jnp.take(jones_all, pick_far, axis=0),
            coords,
            directions,
            brightness,
            seen_block,
            freq_ratio,
        )
        slope_first_antenna = contract(slope_first_antenna, powers)
        slope_second_antenna = contract(slope_second_antenna, powers)
        return (
            resid_block,
            slope_first_antenna.reshape(entries_in_tile, -1),
            slope_second_antenna.reshape(entries_in_tile, -1),
        )

    residual_blocks, slope_first_antenna, slope_second_antenna = lax.map(
        visit_block, (coords_blocks, seen_blocks, near_blocks, far_blocks)
    )
    slope_first_antenna = slope_first_antenna.reshape(pairs_held_here, slope_first_antenna.shape[2])
    slope_second_antenna = slope_second_antenna.reshape(
        pairs_held_here, slope_second_antenna.shape[2]
    )
    summed = lax.psum_scatter(
        segment_rows(slope_first_antenna, station_pair[0], lax.axis_size("stn") * stations_dev)
        + segment_rows(slope_second_antenna, station_pair[1], lax.axis_size("stn") * stations_dev),
        "stn",
        scatter_dimension=0,
        tiled=True,
    )
    gradient = summed.reshape(stations_dev, degree_count * 8, dir_count)
    residual = jnp.transpose(residual_blocks, (1, 2, 0, 3)).reshape(
        frequency_number, 8, pairs_held_here
    )
    return (gradient, residual)


def place(n):
    cores = 2 if n % 2 == 0 else 1
    columns = 2 if n % (2 * cores) == 0 else 1
    depth = n // (cores * columns)
    me = lax.axis_index("stn")
    z, rest = lax.div(me, cores * columns), lax.rem(me, cores * columns)
    return depth, columns, cores, z, lax.div(rest, cores), lax.rem(rest, cores)


class Hops:
    def __init__(self, n, send_sem, recv_sem):
        self.depth, self.columns, self.cores, self.z, self.x, self.c = place(n)
        self.send_sem, self.recv_sem = send_sem, recv_sem
        self.copies = {}

    def index(self, dz, dx, dc):
        z = lax.rem(self.z + dz + self.depth, self.depth)
        x = 1 - self.x if dx else self.x
        c = 1 - self.c if dc else self.c
        return (z * self.columns + x) * self.cores + c

    def greet(self):
        barrier = pltpu.get_barrier_semaphore()
        peers = [(d, 0, 0) for d in range(1, self.depth)]
        peers += [(0, 1, 0)] * (self.columns > 1) + [(0, 0, 1)] * (self.cores > 1)
        for peer in peers:
            pl.semaphore_signal(
                barrier, inc=1, device_id={"stn": self.index(*peer)}, device_id_type=MESH
            )
        pl.semaphore_wait(barrier, len(peers))

    def send(self, key, peer, src, dst):
        number = len(self.copies)
        copy = pltpu.make_async_remote_copy(
            src_ref=src,
            dst_ref=dst,
            send_sem=self.send_sem.at[number],
            recv_sem=self.recv_sem.at[number],
            device_id={"stn": self.index(*peer)},
            device_id_type=MESH,
        )
        copy.start()
        self.copies[key] = copy

    def arrived(self, key):
        self.copies[key].wait_recv()

    def settle(self):
        for copy in self.copies.values():
            copy.wait_send()


def gather_kernel(n, own_ref, all_ref, held, send_sem, recv_sem, out_sem):
    hops = Hops(n, send_sem, recv_sem)
    outs = []

    def keep(src, slot):
        out = pltpu.make_async_copy(src, all_ref.at[slot], out_sem.at[len(outs)])
        out.start()
        outs.append(out)

    me = hops.index(0, 0, 0)
    mine = held.at[me]
    hops.greet()
    for d in range(1, hops.depth):
        hops.send(("z", d), (d, 0, 0), own_ref, mine)
    hops.send(("x", 0), (0, 1, 0), own_ref, mine)
    hops.send(("c", 0, 0), (0, 0, 1), own_ref, mine)
    keep(own_ref, me)
    for d in range(1, hops.depth):
        hops.arrived(("z", d))
        slot = hops.index(-d, 0, 0)
        hops.send(("x", d), (0, 1, 0), held.at[slot], held.at[slot])
        hops.send(("c", d, 0), (0, 0, 1), held.at[slot], held.at[slot])
        keep(held.at[slot], slot)
    for d in range(hops.depth):
        hops.arrived(("x", d))
        slot = hops.index(-d, 1, 0)
        hops.send(("c", d, 1), (0, 0, 1), held.at[slot], held.at[slot])
        keep(held.at[slot], slot)
    for dx in range(2):
        for d in range(hops.depth):
            hops.arrived(("c", d, dx))
            slot = hops.index(-d, dx, 1)
            keep(held.at[slot], slot)
    for out in outs:
        out.wait()
    hops.settle()


def scatter_sum_kernel(n, part_ref, sum_ref, own, from_c, from_x, from_z, send_sem, recv_sem, in_sem):
    hops = Hops(n, send_sem, recv_sem)
    order = [(d, dx) for dx in (1, 0) for d in [*range(1, hops.depth), 0]]
    ins = {}
    for k, (d, dx) in enumerate(order):
        ins[d, dx] = pltpu.make_async_copy(
            part_ref.at[hops.index(d, dx, 0)], own.at[dx, d], in_sem.at[k]
        )
        ins[d, dx].start()
    hops.greet()
    for d, dx in order:
        hops.send(
            ("c", d, dx), (0, 0, 1), part_ref.at[hops.index(d, dx, 1)], from_c.at[dx, d]
        )
    for d, dx in order:
        ins[d, dx].wait()
        hops.arrived(("c", d, dx))
        if dx:
            own[dx, d] = own[dx, d] + from_c[dx, d]
            hops.send(("x", d), (0, 1, 0), own.at[dx, d], from_x.at[d])
            continue
        hops.arrived(("x", d))
        total = own[dx, d] + from_c[dx, d] + from_x[d]
        if d:
            own[dx, d] = total
            hops.send(("z", d), (d, 0, 0), own.at[dx, d], from_z.at[d])
    for d in range(1, hops.depth):
        hops.arrived(("z", d))
        total = total + from_z[d]
    sum_ref[...] = total
    hops.settle()


def turn_sin_cos(turns):
    x = math.pi * (turns - jnp.round(turns))
    y = x * x
    s = jnp.full_like(y, -1.0 / math.factorial(11))
    for k in (9, 7, 5, 3, 1):
        s = s * y + (1.0 if k % 4 == 1 else -1.0) / math.factorial(k)
    s = s * x
    c = jnp.full_like(y, 1.0 / math.factorial(12))
    for k in (10, 8, 6, 4, 2, 0):
        c = c * y + (1.0 if k % 4 == 0 else -1.0) / math.factorial(k)
    return 2.0 * (s * c), 1.0 - 2.0 * (s * s)


def scaled(er, ei, m):
    return [(er * r - ei * i, er * i + ei * r) for r, i in m]


def scaled_conj(er, ei, m):
    return [(er * r + ei * i, er * i - ei * r) for r, i in m]


def real_times(left, right):
    return [
        left[2 * i] * right[j] + left[2 * i + 1] * right[2 + j] for i in range(2) for j in range(2)
    ]


def flipped(m):
    return [m[0], m[2], m[1], m[3]]


def both(m):
    return [r + i for r, i in m]


def plus(a, b):
    return [x + y for x, y in zip(a, b)]


def minus(a, b):
    return [x - y for x, y in zip(a, b)]


def local_kernel(
    degree_count,
    together,
    uvw_ref,
    pair_hbm,
    dir_ref,
    bright_ref,
    seen_ref,
    coeff_hbm,
    part_hbm,
    resid_ref,
    pair_ref,
    coeff_ref,
    part_ref,
    jones,
    with_b,
    with_badj,
    grads,
    seen,
    diffs,
    forms,
    turns,
    steps,
    pair_sem,
    table_sem,
):
    channels = bright_ref.shape[1]
    stations = coeff_ref.shape[0]
    chunk = stations // table_sem.shape[0]

    def span_of(s):
        return pl.ds(pl.multiple_of(lax.div(s, chunk) * chunk, chunk), chunk)

    def table_in(s):
        return pltpu.make_async_copy(
            coeff_hbm.at[span_of(s)], coeff_ref.at[span_of(s)], table_sem.at[lax.div(s, chunk)]
        )

    def part_out(s):
        return pltpu.make_async_copy(
            part_ref.at[span_of(s)], part_hbm.at[span_of(s)], table_sem.at[lax.div(s, chunk)]
        )

    for k in range(table_sem.shape[0]):
        table_in(k * chunk).start()
    pair_in = pltpu.make_async_copy(pair_hbm, pair_ref, pair_sem)
    pair_in.start()
    pairs = uvw_ref.shape[1]
    groups = channels // ROWS
    tile = (ROWS, LANES)
    f32 = jnp.float32
    row = lax.broadcasted_iota(jnp.int32, tile, 0)
    lane = lax.broadcasted_iota(jnp.int32, tile, 1)
    span = max(channels - 1, 1)
    xs = [(2.0 * (row + ROWS * g).astype(f32) - (channels - 1)) / span for g in range(groups)]
    ratio = 1.0 + 0.25 * xs[0]
    stride = 0.25 * 2.0 * ROWS / span

    def block(ref, g, lead=()):
        return [
            tuple(
                ref[(*lead, 2 * e + t, pl.ds(ROWS * g, ROWS), slice(None))] for t in range(2)
            )
            for e in range(4)
        ]

    for g in range(groups):
        for comp in range(8):
            seen[comp, pl.ds(ROWS * g, ROWS), :] = seen_ref[
                pl.ds(8 * ROWS * g + comp, ROWS, stride=8), :
            ]
        for e, (re, im) in enumerate(block(bright_ref, g)):
            forms[e, pl.ds(ROWS * g, ROWS), :] = re + im
            forms[4 + e, pl.ds(ROWS * g, ROWS), :] = re - im

    def prepare(s, carry):
        @pl.when(lax.rem(s, chunk) == 0)
        def _():
            table_in(s).wait()

        table = [
            jnp.broadcast_to(coeff_ref[s, pl.ds(i, 1), :], tile) for i in range(8 * degree_count)
        ]
        for g in range(groups):
            rows = pl.ds(ROWS * g, ROWS)
            flat = []
            for comp in range(8):
                value = table[8 * (degree_count - 1) + comp]
                for n in range(degree_count - 2, -1, -1):
                    value = value * xs[g] + table[8 * n + comp]
                flat.append(value)
            jr, ji = flat[0::2], flat[1::2]
            js = plus(jr, ji)
            br, bi = [bright_ref[2 * e, rows, :] for e in range(4)], [
                bright_ref[2 * e + 1, rows, :] for e in range(4)
            ]
            bs, bd = [forms[e, rows, :] for e in range(4)], [
                forms[4 + e, rows, :] for e in range(4)
            ]
            common = real_times(js, br)
            a = (minus(common, real_times(ji, bs)), minus(common, real_times(jr, bd)))
            common = real_times(js, flipped(br))
            d = (
                minus(common, real_times(ji, flipped(bd))),
                minus(common, real_times(jr, flipped(bs))),
            )
            jd = minus(jr, ji)
            for e in range(4):
                for t in range(2):
                    with_b[s, 2 * e + t, rows, :] = a[t][e]
                    with_badj[s, 2 * e + t, rows, :] = d[t][e]
                for t, form in enumerate((jr, js, jd)):
                    jones[s, 4 * t + e, rows, :] = form[e]
                    if t < 2:
                        grads[s, 4 * t + e, rows, :] = jnp.zeros(tile, f32)
        return carry

    lax.fori_loop(0, stations, prepare, 0)
    pair_in.wait()

    l = jnp.broadcast_to(dir_ref[0:1, :], tile)
    m = jnp.broadcast_to(dir_ref[1:2, :], tile)
    depth = jnp.sqrt(1.0 - l * l - m * m) - 1.0

    def measure(b, carry):
        inner = uvw_ref[0, b] * l + uvw_ref[1, b] * m + uvw_ref[2, b] * depth
        turns[pl.ds(b, 1), :] = inner[0:1, :]
        return carry

    lax.fori_loop(0, pairs, measure, 0, unroll=8)

    def step_of(i, carry):
        some = pl.ds(pl.multiple_of(i * ROWS, ROWS), ROWS)
        s, c = turn_sin_cos(stride * turns[some, :])
        steps[0, some, :] = s
        steps[1, some, :] = c
        return carry

    lax.fori_loop(0, pairs // ROWS, step_of, 0)

    def predict(b):
        p, q = pair_ref[0, b], pair_ref[1, b]
        s, c = turn_sin_cos(ratio * jnp.broadcast_to(turns[pl.ds(b, 1), :], tile))
        step_s = jnp.broadcast_to(steps[0, pl.ds(b, 1), :], tile)
        step_c = jnp.broadcast_to(steps[1, pl.ds(b, 1), :], tile)
        er, ei = c, -s
        here = lane == b
        out = []
        for g in range(groups):
            rows = pl.ds(ROWS * g, ROWS)
            if g:
                er, ei = er * step_c + ei * step_s, ei * step_c - er * step_s
            t = scaled(er, ei, block(with_b, g, (p,)))
            tr, ti = [v[0] for v in t], [v[1] for v in t]
            ts = plus(tr, ti)
            jr, js, jd = [
                flipped([jones[q, 4 * k + e, rows, :] for e in range(4)]) for k in range(3)
            ]
            common = real_times(ts, jr)
            model = (minus(common, real_times(ti, jd)), minus(common, real_times(tr, js)))
            diff = ([], [])
            for e in range(4):
                for k in range(2):
                    comp = 2 * e + k
                    term = model[k][e] - jnp.where(here, seen[comp, rows, :], 0.0)
                    total = jnp.broadcast_to(jnp.sum(term, axis=1, keepdims=True), tile)
                    pltpu.store(diffs.at[comp, rows, :], total, mask=here)
                    diff[k].append(total)
            out.append((er, ei, tr, ti, ts, diff))
        return p, q, out

    def deposit(state):
        p, q, out = state
        for g in range(groups):
            rows = pl.ds(ROWS * g, ROWS)
            er, ei, tr, ti, ts, (rr, ri) = out[g]
            u = scaled_conj(er, ei, block(with_badj, g, (q,)))
            ur, ui = [v[0] for v in u], [v[1] for v in u]
            rp, rm = plus(rr, ri), minus(ri, rr)
            near = (real_times(rr, both(u)), real_times(rp, ui), real_times(rm, ur))
            near = (minus(near[0], near[1]), plus(near[0], near[2]))
            for k in range(2):
                for e in range(4):
                    grads[p, 4 * k + e, rows, :] += near[k][e]
            far = (
                real_times(flipped(rr), ts),
                real_times(flipped(rm), ti),
                real_times(flipped(rp), tr),
            )
            far = (plus(far[0], far[1]), minus(far[0], far[2]))
            for k in range(2):
                for e in range(4):
                    grads[q, 4 * k + e, rows, :] += far[k][e]

    def visit(i, carry):
        last = predict(i * together)
        for u in range(1, together):
            state = predict(i * together + u)
            deposit(last)
            last = state
        deposit(last)
        return carry

    lax.fori_loop(0, pairs // together, visit, 0)

    def finish(s, carry):
        for comp in range(8):
            slot = 4 * (comp % 2) + comp // 2
            terms = [grads[s, slot, pl.ds(ROWS * g, ROWS), :] for g in range(groups)]
            for n in range(degree_count):
                if n:
                    terms = [v * x for v, x in zip(terms, xs)]
                part_ref[s, pl.ds(8 * n + comp, 1), :] = jnp.sum(
                    sum(terms[1:], terms[0]), axis=0, keepdims=True
                )

        @pl.when(lax.rem(s, chunk) == chunk - 1)
        def _():
            part_out(s).start()

        return carry

    lax.fori_loop(0, stations, finish, 0)

    for g in range(groups):
        for comp in range(8):
            resid_ref[pl.ds(8 * ROWS * g + comp, ROWS, stride=8), :] = -diffs[
                comp, pl.ds(ROWS * g, ROWS), :
            ]
    for k in range(table_sem.shape[0]):
        part_out(k * chunk).wait()


def gather(own, n):
    return pl.pallas_call(
        functools.partial(gather_kernel, n),
        out_shape=jax.ShapeDtypeStruct((n, *own.shape), own.dtype),
        in_specs=[pl.BlockSpec(memory_space=pltpu.VMEM)],
        out_specs=pl.BlockSpec(memory_space=pltpu.HBM),
        scratch_shapes=[
            pltpu.VMEM((n, *own.shape), own.dtype),
            pltpu.SemaphoreType.DMA((n,)),
            pltpu.SemaphoreType.DMA((n,)),
            pltpu.SemaphoreType.DMA((n,)),
        ],
        compiler_params=pltpu.CompilerParams(collective_id=1, has_side_effects=True, vmem_limit_bytes=VMEM_BUDGET),
        name="gather_coefficients",
    )(own)


def scatter_sum(parts, n):
    piece = parts.shape[1:]
    return pl.pallas_call(
        functools.partial(scatter_sum_kernel, n),
        out_shape=jax.ShapeDtypeStruct(piece, parts.dtype),
        in_specs=[pl.BlockSpec(memory_space=pltpu.HBM)],
        out_specs=pl.BlockSpec(memory_space=pltpu.VMEM),
        scratch_shapes=[
            pltpu.VMEM((2, n // 4, *piece), parts.dtype),
            pltpu.VMEM((2, n // 4, *piece), parts.dtype),
            pltpu.VMEM((n // 4, *piece), parts.dtype),
            pltpu.VMEM((n // 4, *piece), parts.dtype),
            pltpu.SemaphoreType.DMA((n,)),
            pltpu.SemaphoreType.DMA((n,)),
            pltpu.SemaphoreType.DMA((n,)),
        ],
        compiler_params=pltpu.CompilerParams(collective_id=2, has_side_effects=True, vmem_limit_bytes=VMEM_BUDGET),
        name="sum_gradient",
    )(parts)


def compact_shards(uvw, directions, brightness, observed, coefficients, pair):
    n = lax.axis_size("stn")
    channels, dirs = brightness.shape[1:]
    held, rows = coefficients.shape[:2]
    pairs = uvw.shape[1]
    table = gather(coefficients, n).reshape(n * held, rows, dirs)
    vmem = pl.BlockSpec(memory_space=pltpu.VMEM)
    away = pl.BlockSpec(memory_space=pltpu.HBM)
    smem = pl.BlockSpec(memory_space=pltpu.SMEM)

    def per_station(forms):
        return pltpu.VMEM((n * held, forms, channels, dirs), jnp.float32)

    per_pair = pltpu.VMEM((8, channels, pairs), jnp.float32)
    partial, residual = pl.pallas_call(
        functools.partial(local_kernel, rows // 8, 4),
        out_shape=(
            jax.ShapeDtypeStruct(table.shape, jnp.float32),
            jax.ShapeDtypeStruct((channels * 8, pairs), jnp.float32),
        ),
        in_specs=[smem, away, vmem, vmem, vmem, away],
        out_specs=(away, vmem),
        scratch_shapes=[pltpu.SMEM(pair.shape, pair.dtype)]
        + [pltpu.VMEM(table.shape, jnp.float32)] * 2
        + [per_station(12), per_station(8), per_station(8), per_station(8)]
        + [per_pair] * 2
        + [
            pltpu.VMEM((8, channels, dirs), jnp.float32),
            pltpu.VMEM((pairs, dirs), jnp.float32),
            pltpu.VMEM((2, pairs, dirs), jnp.float32),
        ]
        + [pltpu.SemaphoreType.DMA, pltpu.SemaphoreType.DMA((4,))],
        compiler_params=pltpu.CompilerParams(vmem_limit_bytes=VMEM_BUDGET),
        name="predict_and_slope",
    )(uvw, pair, directions, brightness, observed.reshape(channels * 8, pairs), table)
    gradient = scatter_sum(partial.reshape(n, held, rows, dirs), n)
    return gradient, residual.reshape(channels, 8, pairs)


def shards(uvw, directions, brightness, observed, coefficients, pair):
    channels, dirs = brightness.shape[1:]
    stations = lax.axis_size("stn") * coefficients.shape[0]
    fits = lax.axis_size("stn") % 4 == 0 and 36 * stations * channels * dirs * 4 <= 22 * 1024 * 1024
    if fits and dirs == LANES and uvw.shape[1] == LANES and channels % ROWS == 0:
        return compact_shards(uvw, directions, brightness, observed, coefficients, pair)
    return general_shards(uvw, directions, brightness, observed, coefficients, pair)


def solution(mesh):
    placed = (
        P(None, ("grp", "stn")),
        P(),
        P(),
        P(None, None, ("grp", "stn")),
        P(("grp", "stn"), None, None),
        P(None, ("grp", "stn")),
    )
    return jax.shard_map(
        shards,
        mesh=mesh,
        in_specs=placed,
        out_specs=(P(("grp", "stn"), None, None), P(None, None, ("grp", "stn"))),
        check_vma=False,
    )
```
